128 devices in a mesh: seq: 32 (over y, z, core), head: 4 (over x).
Axes of the slice: x: 4, y: 4, z: 4, core: 2. Of those that a mesh axis runs over, the one named last changes fastest.
Arguments:
- tile_features: bfloat16 [81920, 768], P(('seq', 'head')), may hold values from -40 to 40
- kept_tiles: int32 [32768], P('seq'), may hold values from 0 to 81919, as said below
- attn_gain: float32 [768], replicated, may hold values from 0.1 to 1.9
- qkv_weight: bfloat16 [768, 3, 768], P(None, None, 'head'), may hold values from -4 to 4
- out_weight: bfloat16 [768, 768], P('head'), may hold values from -0.21875 to 0.21875
- middle_head_offset: int32 [12], P('head'), may hold values from 0 to 3
- far_head_offset: int32 [12], P('head'), may hold values from 0 to 15
- mlp_gain: float32 [768], replicated, may hold values from 0.1 to 1.9
- up_weight: bfloat16 [768, 3072], P(None, 'head'), may hold values from -0.21875 to 0.21875
- down_weight: bfloat16 [3072, 768], P('head'), may hold values from -0.109375 to 0.109375
Outputs:
- encoded: bfloat16 [32768, 768], P(('seq', 'head'))
The draws below stay inside these ranges and needn't reach their ends.
Inputs may be any that keep to these rules, and one draw needn't show every extreme that they name: `kept_tiles`: strictly increasing. For every d < 32, entry (d + 1) * 1024 - 1 minus entry d * 1024 is at most 2047, and equals it for some d.
All inputs are finite; a program needn't handle non-finite values.
Results may differ from the reference program's by a relative error of at most 0.014.
Values may be sent and summed in bfloat16 or wider, within the bound.
A program may use at most 64 MiB of HBM per device.

```python
import math
import jax
import jax.numpy as jnp
from jax import lax

D = 768
HEAD_NUMBER = 12
HD = 64
FF = 3072
KD = 1024
MIDDLE_DILATION = 4
FAR_DILATION = 16
SHORT_SEG = 1024
MIDDLE_SEGMENT = 4096
KEPT_TILES = 32768
FAR_SEGMENT = 32768
SPAN = 2048
TILES = 81920
N_SEQ = 32
N_HEAD = 4


def draw_tile_features(key, part):
    key = jax.random.fold_in(key, 11)
    drawn = jax.random.normal(key, (TILES, D), jnp.float32)
    drawn = jnp.clip(drawn, -6.0, 6.0)
    return jnp.clip(drawn, -40.0, 40.0).astype(jnp.bfloat16)


def draw_kept_tiles(key, part):
    key = jax.random.fold_in(key, 23)
    extent_key, widest_key, spacing_key, place_key = jax.random.split(key, 4)
    extents = jax.random.randint(extent_key, (N_SEQ,), KD, SPAN + 1)
    widest = jax.random.randint(widest_key, (), 0, N_SEQ)
    extents = jnp.where(jnp.arange(N_SEQ) == widest, SPAN, extents).astype(jnp.int32)
    spare = TILES - jnp.sum(extents)
    shares = jax.random.randint(spacing_key, (N_SEQ + 1,), 1, 101)
    spacing = spare * shares // jnp.sum(shares)
    starts = jnp.cumsum(spacing[:N_SEQ]) + jnp.cumsum(extents) - extents

    def one_block(block_key, first_place, extent):
        positions = jnp.arange(SPAN, dtype=jnp.int32)
        ranking = jax.random.randint(block_key, (SPAN,), 0, 32768) * SPAN + positions
        interior = (positions >= 1) & (positions <= extent - 2)
        ranking = jnp.where(interior, ranking, 2 ** 30 + positions)
        scored, chosen = lax.top_k(-ranking, KD - 2)
        edges = jnp.stack([jnp.zeros((), jnp.int32), (extent - 1).astype(jnp.int32)])
        offsets = jnp.sort(jnp.concatenate([edges, chosen.astype(jnp.int32)]))
        return first_place + offsets
    block_keys = jax.random.split(place_key, N_SEQ)
    return jax.vmap(one_block)(block_keys, starts, extents).reshape(KEPT_TILES).astype(jnp.int32)


def draw_qkv_weight(key, part):
    key = jax.random.fold_in(key, 37)
    query_key, key_key, value_key = jax.random.split(key, 3)
    scale = 1.7 / math.sqrt(D)
    query_part = jax.random.normal(query_key, (D, 1, HEAD_NUMBER * HD), jnp.float32) * scale
    key_part = jax.random.normal(key_key, (D, 1, HEAD_NUMBER * HD), jnp.float32) * scale
    value_part = jax.random.normal(value_key, (D, 1, HEAD_NUMBER * HD), jnp.float32) / math.sqrt(D)
    drawn = jnp.concatenate([query_part, key_part, value_part], axis=1)
    return jnp.clip(drawn, -4.0, 4.0).astype(jnp.bfloat16)


def with_ends(values, rng, smallest, high):
    longest = values.shape.index(max(values.shape))
    spots = []
    for shift in (0, 1):
        where = [jax.random.randint(jax.random.fold_in(rng, axis), (), 0, length) for axis, length in enumerate(values.shape)]
        where[longest] = (where[longest] + shift) % values.shape[longest]
        spots.append(tuple(where))
    return values.at[spots[0]].set(smallest).at[spots[1]].set(high)


def block_levels(stream_key, shape, pieces, smallest, top_value):
    level, own = 1.0, jax.random.fold_in(stream_key, 6)
    for axis_at, blocks in pieces:
        steps = jnp.exp(jax.random.uniform(jax.random.fold_in(own, axis_at), (blocks,), jnp.float32, smallest / len(pieces), top_value / len(pieces)))
        level = level * jnp.repeat(steps, shape[axis_at] // blocks).reshape([-1 if axis == axis_at else 1 for axis in range(len(shape))])
    return level


def gaussian(own_key, shape, scale, bound, pieces=(), kind=jnp.bfloat16):
    result = scale * jax.random.normal(own_key, shape, jnp.float32)
    if pieces:
        result = result * block_levels(own_key, shape, pieces, -0.22, 0.18)
    return jnp.clip(result, -bound, bound).astype(kind)


def setup_inputs(seed: int = 0) -> dict:
    arg_keys = jax.random.split(jax.random.key(seed), 11)
    tile_features = draw_tile_features(jax.random.fold_in(arg_keys[10], 71), 0)
    kept_tiles = draw_kept_tiles(jax.random.fold_in(arg_keys[10], 71), 0)
    attn_gain = jnp.clip(1.0 + 0.18 * jax.random.normal(arg_keys[2], (D,), jnp.float32), 0.1, 1.9)
    qkv_weight = draw_qkv_weight(jax.random.fold_in(arg_keys[10], 71), 0)
    out_weight = gaussian(arg_keys[4], (HEAD_NUMBER * HD, D), (HEAD_NUMBER * HD) ** -0.5, 0.21875, ((0, 4),))
    middle_head_offset = with_ends(jax.random.randint(arg_keys[5], (HEAD_NUMBER,), 0, MIDDLE_DILATION), jax.random.fold_in(arg_keys[5], 1), 0, MIDDLE_DILATION - 1).astype(jnp.int32)
    far_head_offset = with_ends(jax.random.randint(arg_keys[6], (HEAD_NUMBER,), 0, FAR_DILATION), jax.random.fold_in(arg_keys[6], 1), 0, FAR_DILATION - 1).astype(jnp.int32)
    mlp_gain = jnp.clip(1.0 + 0.18 * jax.random.normal(arg_keys[7], (D,), jnp.float32), 0.1, 1.9)
    up_weight = gaussian(arg_keys[8], (D, FF), D ** -0.5, 0.21875, ((1, 4),))
    down_weight = gaussian(arg_keys[9], (FF, D), FF ** -0.5, 0.109375, ((0, 4),))
    return {"tile_features": tile_features, "kept_tiles": kept_tiles, "attn_gain": attn_gain, "qkv_weight": qkv_weight, "out_weight": out_weight, "middle_head_offset": middle_head_offset, "far_head_offset": far_head_offset, "mlp_gain": mlp_gain, "up_weight": up_weight, "down_weight": down_weight}


EPSILON = 1e-05
VERY_NEGATIVE = -1e+30

def layer_norm(row_block, gain):
    row_block = row_block.astype(jnp.float32)
    centred = row_block - lax.optimization_barrier(jnp.mean(row_block, axis=-1, keepdims=True))
    variance = lax.optimization_barrier(jnp.mean(centred * centred, axis=-1, keepdims=True))
    return centred * lax.rsqrt(variance + EPSILON) * gain

def apply_attention(query_rows, key_matrix, value_rows):
    score_scale = 1.0 / math.sqrt(HD)
    scores = jnp.einsum('hqd,hkd->hqk', query_rows.astype(jnp.float32), key_matrix.astype(jnp.float32), precision=lax.Precision.HIGHEST) * score_scale
    highest = lax.optimization_barrier(jnp.max(scores, axis=-1))
    weights = jnp.exp(scores - highest[..., None])
    summed = lax.optimization_barrier(jnp.sum(weights, axis=-1))
    rounded = lax.optimization_barrier(weights.astype(jnp.bfloat16)).astype(jnp.float32)
    weighted = jnp.einsum('hqk,hkd->hqd', rounded, value_rows.astype(jnp.float32), precision=lax.Precision.HIGHEST)
    return (weighted, highest, summed)

def select_rows(row_block, offset, dilation):
    lattice = row_block.reshape(row_block.shape[0] // dilation, dilation, offset.shape[0], -1)
    cell_mask = jnp.arange(dilation)[:, None] == offset[None, :]
    return lax.optimization_barrier(jnp.sum(jnp.where(cell_mask[None, :, :, None], lattice, jnp.zeros((), row_block.dtype)), axis=1))

def widen_rows(weighted, highest, summed, offset, dilation):
    head_number, row_count = highest.shape
    cell_mask = jnp.arange(dilation)[None, :] == offset[:, None]
    highest = jnp.where(cell_mask[:, None, :], highest[:, :, None], VERY_NEGATIVE).reshape(head_number, row_count * dilation)
    summed = jnp.where(cell_mask[:, None, :], summed[:, :, None], 0.0).reshape(head_number, row_count * dilation)
    weighted = jnp.where(cell_mask[:, None, :, None], weighted[:, :, None, :], 0.0).reshape(head_number, row_count * dilation, -1)
    return (weighted, highest, summed)

def segment_attend(row_triple):
    query_rows, key_matrix, value_rows = row_triple
    return apply_attention(query_rows.transpose(1, 0, 2), key_matrix.transpose(1, 0, 2), value_rows.transpose(1, 0, 2))

def segment_split(query_rows, key_matrix, value_rows, segments):
    row_count = query_rows.shape[0] // segments
    shaped = (query_rows.reshape(segments, row_count, HEAD_NUMBER, HD), key_matrix.reshape(segments, row_count, HEAD_NUMBER, HD), value_rows.reshape(segments, row_count, HEAD_NUMBER, HD))
    weighted, highest, summed = lax.map(segment_attend, shaped)
    weighted = weighted.transpose(1, 0, 2, 3).reshape(HEAD_NUMBER, segments * row_count, HD)
    highest = highest.transpose(1, 0, 2).reshape(HEAD_NUMBER, segments * row_count)
    summed = summed.transpose(1, 0, 2).reshape(HEAD_NUMBER, segments * row_count)
    return (weighted, highest, summed)

def grouped_sum(left_side, right_side):
    group_width = left_side.shape[1] // N_HEAD
    summed = jnp.zeros((left_side.shape[0], right_side.shape[1]), jnp.float32)
    for group_index in range(N_HEAD):
        partial_product = jnp.dot(left_side[:, group_index * group_width:(group_index + 1) * group_width], right_side[group_index * group_width:(group_index + 1) * group_width], preferred_element_type=jnp.float32)
        summed = summed + lax.optimization_barrier(partial_product.astype(jnp.bfloat16)).astype(jnp.float32)
    return summed

def reference(tile_features, kept_tiles, attn_gain, qkv_weight, out_weight, middle_head_offset, far_head_offset, mlp_gain, up_weight, down_weight):
    devices = N_SEQ * N_HEAD
    rows_at = (kept_tiles % devices * (TILES // devices) + kept_tiles // devices).astype(jnp.int32)
    dense_rows = jnp.take(tile_features, rows_at, axis=0)
    normed = layer_norm(dense_rows, attn_gain).astype(jnp.bfloat16)
    projected = jnp.dot(normed, qkv_weight.reshape(D, 3 * HEAD_NUMBER * HD), preferred_element_type=jnp.float32).astype(jnp.bfloat16)
    projected = projected.reshape(KEPT_TILES, 3, HEAD_NUMBER, HD)
    query_rows = projected[:, 0]
    key_matrix = projected[:, 1]
    value_rows = projected[:, 2]
    weighted_one, highest_one, summed_one = segment_split(query_rows, key_matrix, value_rows, KEPT_TILES // SHORT_SEG)
    middle_output = segment_split(select_rows(query_rows, middle_head_offset, MIDDLE_DILATION), select_rows(key_matrix, middle_head_offset, MIDDLE_DILATION), select_rows(value_rows, middle_head_offset, MIDDLE_DILATION), KEPT_TILES // MIDDLE_SEGMENT)
    weighted_sum_two, maximum_two, total_two = widen_rows(middle_output[0], middle_output[1], middle_output[2], middle_head_offset, MIDDLE_DILATION)
    far_output = segment_split(select_rows(query_rows, far_head_offset, FAR_DILATION), select_rows(key_matrix, far_head_offset, FAR_DILATION), select_rows(value_rows, far_head_offset, FAR_DILATION), KEPT_TILES // FAR_SEGMENT)
    weighted_sum_three, maximum_three, total_three = widen_rows(far_output[0], far_output[1], far_output[2], far_head_offset, FAR_DILATION)
    largest = jnp.maximum(jnp.maximum(highest_one, maximum_two), maximum_three)
    scale_one = jnp.exp(highest_one - largest)
    scale_two = jnp.exp(maximum_two - largest)
    scale_three = jnp.exp(maximum_three - largest)
    numerator = scale_one[..., None] * weighted_one + scale_two[..., None] * weighted_sum_two + scale_three[..., None] * weighted_sum_three
    denominator = scale_one * summed_one + scale_two * total_two + scale_three * total_three
    merged = numerator / denominator[..., None]
    heads_out = merged.transpose(1, 0, 2).reshape(KEPT_TILES, HEAD_NUMBER * HD).astype(jnp.bfloat16)
    residual = dense_rows.astype(jnp.float32) + grouped_sum(heads_out, out_weight)
    normed_two = layer_norm(residual, mlp_gain).astype(jnp.bfloat16)
    hidden = jax.nn.gelu(jnp.dot(normed_two, up_weight, preferred_element_type=jnp.float32), approximate=False).astype(jnp.bfloat16)
    return (residual + grouped_sum(hidden, down_weight)).astype(jnp.bfloat16)
```

```python
import functools

import jax
import jax.numpy as jnp
from jax import lax
from jax.experimental import pallas as pl
from jax.experimental.pallas import tpu as pltpu
from jax.sharding import PartitionSpec as P

NS = 32
NH = 4
ND = NS * NH
D = 768
KD = 1024
HD = 64
HPD = 3
WIN = 16
ROWS = 640
SHARE = KD // NH
EPS = 1e-05
NEG = -1e30
BF = jnp.bfloat16
F32 = jnp.float32


def dot(a, b):
    return lax.dot_general(a, b, (((1,), (0,)), ((), ())), preferred_element_type=F32)


def dot_nt(a, b):
    return lax.dot_general(a, b, (((1,), (1,)), ((), ())), preferred_element_type=F32)


def layer_norm(x, gain):
    centred = x - jnp.mean(x, axis=-1, keepdims=True)
    variance = jnp.mean(centred * centred, axis=-1, keepdims=True)
    return centred * lax.rsqrt(variance + EPS) * gain


def iota(shape, axis):
    return lax.broadcasted_iota(jnp.int32, shape, axis)


def v_first(head):
    return head != 1


def kernel(
    kept_s, moff, foff, kept_c, feat, again, wqkv, mgain, up, down, outw,
    o_ref,
    send, recv, slot, dense, q, kv, qmid, qfar, midkv, farkv, acc, accm, accf,
    ho_send, ho_recv, fk_send, fk_recv, upf, downf, outf,
    fk_ss, fk_rs, s1_ss, s1_rs, xs, xr, ws, wr, wl, ms, mr, fs, fr, hs, hr,
):
    me = lax.axis_index("seq")
    h = lax.axis_index("head")
    right, left, opp = (h + 1) % NH, (h + 3) % NH, (h + 2) % NH
    core = me % 2
    chip = me // 2
    sib = me + 1 - 2 * core
    zbit = chip % 2
    zpart = me + 2 - 4 * zbit
    source = me * NH + h

    def rcopy(src, dst, ssem, rsem, seq, head):
        return pltpu.make_async_remote_copy(
            src_ref=src, dst_ref=dst, send_sem=ssem, recv_sem=rsem,
            device_id=(seq, head), device_id_type=pl.DeviceIdType.MESH,
        )

    barrier = pltpu.get_barrier_semaphore()

    def greet(i, c):
        pl.semaphore_signal(barrier, inc=1, device_id=((me + i) % NS, h), device_id_type=pl.DeviceIdType.MESH)
        return c

    lax.fori_loop(1, NS, greet, 0)
    for other in (right, left, opp):
        pl.semaphore_signal(barrier, inc=1, device_id=(me, other), device_id_type=pl.DeviceIdType.MESH)
    first = kept_s[0]
    fk_send[...] = jnp.full((8, 128), first, jnp.int32)
    fk_recv[0] = fk_send[...]
    pl.semaphore_wait(barrier, NS - 1 + NH - 1)

    def send_first(i, c):
        rcopy(fk_send, fk_recv.at[NS - i], fk_ss, fk_rs, (me + i) % NS, h).start()
        return c

    lax.fori_loop(1, NS, send_first, 0)

    weights = []
    for a, (inp, full) in enumerate(((outw, outf), (up, upf), (down, downf))):
        n = inp.shape[0]
        half, quarter = n // 2, n // 4
        lo = pl.multiple_of(core * half, 16)
        mid = pl.multiple_of(core * half + quarter, 16)
        own = pl.ds(lo, half)
        src = inp.at[own]
        local = pltpu.make_async_copy(inp, full.at[h], wl.at[a])
        mine = [
            rcopy(src, full.at[h, own], ws.at[a, 0], wr.at[a, 0], me, right),
            rcopy(src, full.at[h, own], ws.at[a, 1], wr.at[a, 1], me, left),
        ]
        ahead = [
            rcopy(full.at[left, pl.ds(lo, quarter)], full.at[left, pl.ds(lo, quarter)], ws.at[a, 2], wr.at[a, 2], me, right),
            rcopy(full.at[right, pl.ds(mid, quarter)], full.at[right, pl.ds(mid, quarter)], ws.at[a, 3], wr.at[a, 3], me, left),
        ]
        twin = [
            rcopy(full.at[left, own], full.at[left, own], ws.at[a, 4], wr.at[a, 4], sib, h),
            rcopy(full.at[right, own], full.at[right, own], ws.at[a, 5], wr.at[a, 5], sib, h),
            rcopy(full.at[opp, own], full.at[opp, own], ws.at[a, 6], wr.at[a, 6], sib, h),
        ]
        weights.append((local, mine, ahead, twin))

    def weights_start(a):
        local, mine, _, _ = weights[a]
        local.start()
        mine[0].start()
        mine[1].start()

    def weights_pass(a):
        _, mine, ahead, twin = weights[a]
        for k in range(2):
            mine[k].wait_recv()
            ahead[k].start()
            twin[k].start()

    def weights_last(a):
        _, _, ahead, twin = weights[a]
        ahead[0].wait_recv()
        ahead[1].wait_recv()
        twin[2].start()

    def weights_done(a):
        local, mine, ahead, twin = weights[a]
        for t in twin:
            t.wait_recv()
        local.wait()
        for t in mine + ahead + twin:
            t.wait_send()

    weights_start(0)

    kc = kept_c[...]
    sender = kc & (ND - 1)
    s_seq, s_head = lax.shift_right_arithmetic(sender, 2), sender & (NH - 1)
    within = lax.shift_right_arithmetic(kc, 7) - lax.shift_right_arithmetic(first - sender + (ND - 1), 7)
    rel = (me - s_seq + NS) & (NS - 1)
    slot[...] = (lax.shift_right_arithmetic(rel, 3) * 32 + s_head * 8 + (rel & 7)) * WIN + within

    all_first = rcopy(fk_recv.at[pl.ds(1, NS - 1)], fk_recv.at[pl.ds(1, NS - 1)], fk_ss, fk_rs, me, right)
    all_first.wait_recv()

    def send_windows(g, c):
        firsts = fk_recv[pl.ds(pl.multiple_of(g * 8, 8), 8)]
        start = lax.shift_right_arithmetic(firsts - source + (ND - 1), 7)
        start = jnp.concatenate([start, start], axis=1).reshape(128, 128)
        want = start + iota((128, 128), 0) % WIN - iota((128, 128), 1)
        pick = jnp.concatenate(
            [(want == t * 128).astype(F32).astype(BF) for t in range(ROWS // 128)], axis=1
        )
        send[pl.ds(pl.multiple_of(g * 128, 128), 128)] = dot(pick, feat[...]).astype(BF)

        def one(i, c):
            at = pl.ds(pl.multiple_of(g * 128 + i * WIN, WIN), WIN)
            rcopy(
                send.at[at], recv.at[g, h, pl.ds(pl.multiple_of(i * WIN, WIN), WIN)],
                s1_ss, s1_rs.at[g], (me + g * 8 + i) % NS, h,
            ).start()
            return c

        lax.fori_loop(jnp.where(g == 0, 1, 0), 8, one, 0)
        return c

    lax.fori_loop(0, 4, send_windows, 0)
    recv[0, h, 0:WIN] = send[0:WIN]

    def arrive(g):
        lo = WIN if g == 0 else 0
        part = recv.at[g, h, pl.ds(lo, 128 - lo)]
        rcopy(part, part, s1_ss, s1_rs.at[g], me, right).wait_recv()

    rings = []
    for g in range(4):
        rings.append((
            rcopy(recv.at[g, h], recv.at[g, h], xs.at[g, 0], xr.at[g, 0], me, right),
            rcopy(recv.at[g, h], recv.at[g, h], xs.at[g, 1], xr.at[g, 1], me, left),
            rcopy(recv.at[g, left, pl.ds(0, 64)], recv.at[g, left, pl.ds(0, 64)], xs.at[g, 2], xr.at[g, 2], me, right),
            rcopy(recv.at[g, right, pl.ds(64, 64)], recv.at[g, right, pl.ds(64, 64)], xs.at[g, 3], xr.at[g, 3], me, left),
        ))

    def compact(g):
        rings[g][2].wait_recv()
        rings[g][3].wait_recv()

        def block(b, c):
            at = pl.ds(pl.multiple_of(b * 256, 256), 256)
            pick = (iota((256, 512), 1) + g * 512 == slot[at]).astype(F32).astype(BF)
            got = dot(pick, recv[g].reshape(512, D))
            if g == 0:
                dense[at] = got
            else:
                dense[at] = dense[at] + got
            return c

        lax.fori_loop(0, KD // 256, block, 0)

    def ring_pass(g):
        rings[g][0].wait_recv()
        rings[g][2].start()
        rings[g][1].wait_recv()
        rings[g][3].start()

    for g in range(4):
        arrive(g)
        rings[g][0].start()
        rings[g][1].start()
        if g >= 1:
            ring_pass(g - 1)
    ring_pass(3)
    weights_pass(0)
    weights_start(1)
    weights_start(2)
    for g in range(4):
        compact(g)
    weights_last(0)

    def project(b, c):
        at = pl.ds(pl.multiple_of(b * 256, 256), 256)
        normed = layer_norm(dense[at], again[...]).astype(BF)
        qb = (dot(normed, wqkv[:, :384]).astype(BF).astype(F32) * 0.125).astype(BF)
        kvb = dot(normed, wqkv[:, 384:]).astype(BF)
        q[at] = qb
        kv[at] = kvb
        at_m = pl.ds(pl.multiple_of(b * 64, 64), 64)
        at_f = pl.ds(pl.multiple_of(b * 16, 16), 16)
        for j in range(HPD):
            cols = slice(j * 128, (j + 1) * 128)
            sel = (iota((64, 256), 1) == iota((64, 256), 0) * 4 + moff[j]).astype(F32).astype(BF)
            midkv[core, zbit, at_m, cols] = dot(sel, kvb[:, cols]).astype(BF)
            qmid[at_m, cols] = dot(sel, qb[:, cols]).astype(BF)
            sel = (iota((16, 256), 1) == iota((16, 256), 0) * 16 + foff[j]).astype(F32).astype(BF)
            farkv[core, chip, at_f, cols] = dot(sel, kvb[:, cols]).astype(BF)
            qfar[at_f, cols] = dot(sel, qb[:, cols]).astype(BF)
        return c

    lax.fori_loop(0, KD // 256, project, 0)

    def send_far(i, c):
        rcopy(farkv.at[core, chip], farkv.at[core, chip], fs.at[0], fr.at[0], (me + 2 * i) % NS, h).start()
        return c

    lax.fori_loop(1, NS // 2, send_far, 0)
    mid_z = rcopy(midkv.at[core, zbit], midkv.at[core, zbit], ms.at[0], mr.at[0], zpart, h)
    mid_z.start()
    mid_s = rcopy(midkv.at[core], midkv.at[core], ms.at[1], mr.at[1], sib, h)
    far_all = rcopy(farkv.at[core, pl.ds(0, 15)], farkv.at[core, pl.ds(0, 15)], fs.at[0], fr.at[0], sib, h)
    far_s = rcopy(farkv.at[core], farkv.at[core], fs.at[1], fr.at[1], sib, h)

    def attend(qb, keys, j):
        scores = dot_nt(qb, keys)
        top = jnp.max(scores, axis=-1, keepdims=True)
        p = jnp.exp(scores - top)
        total = jnp.sum(p, axis=-1, keepdims=True)
        out = dot(p.astype(BF), keys)
        lane = iota(out.shape, 1)
        base = 64 if v_first(j) else 0
        out = jnp.where((lane >= base) & (lane < base + 32), top, out)
        return jnp.where((lane >= base + 32) & (lane < base + 64), total, out)

    for j in range(HPD):
        cols = slice(j * 128, (j + 1) * 128)

        def short(b, c):
            at = pl.ds(pl.multiple_of(b * 256, 256), 256)
            acc[j, at] = attend(q[at, cols], kv[:, cols], j)
            return c

        lax.fori_loop(0, KD // 256, short, 0)
        if j == 0:
            mid_z.wait_recv()
            mid_s.start()
        if j == 1:
            far_all.wait_recv()
            far_s.start()
    weights_pass(1)
    mid_s.wait_recv()
    for j in range(HPD):
        cols = slice(j * 128, (j + 1) * 128)
        accm[j] = attend(qmid[:, cols], midkv[:, :, :, cols].reshape(KD, 128), j)
    far_s.wait_recv()
    for j in range(HPD):
        cols = slice(j * 128, (j + 1) * 128)
        accf[j] = attend(qfar[:, cols], farkv[:, :, :, cols].reshape(2048, 128), j)

    def spread(one_hot, x):
        one = x.astype(BF)
        rest = x - one.astype(F32)
        two = rest.astype(BF)
        three = (rest - two.astype(F32)).astype(BF)
        return dot(one_hot, one) + dot(one_hot, two) + dot(one_hot, three)

    def merge(g):
        heads = []
        at = pl.ds(pl.multiple_of(g * 256, 256), 256)
        at_m = pl.ds(pl.multiple_of(g * 64, 64), 64)
        at_f = pl.ds(pl.multiple_of(g * 16, 16), 16)
        for j in range(HPD):
            base = 64 if v_first(j) else 0
            near = acc[j, at]
            hot_m = (iota((256, 64), 0) == iota((256, 64), 1) * 4 + moff[j]).astype(F32).astype(BF)
            hot_f = (iota((256, 16), 0) == iota((256, 16), 1) * 16 + foff[j]).astype(F32).astype(BF)
            middle = spread(hot_m, accm[j, at_m])
            far = spread(hot_f, accf[j, at_f])
            pos = iota((256, 1), 0)
            in_m = pos % 4 == moff[j]
            in_f = pos % 16 == foff[j]
            top_n = near[:, base:base + 1]
            top_m = jnp.where(in_m, middle[:, base:base + 1], NEG)
            top_f = jnp.where(in_f, far[:, base:base + 1], NEG)
            top = jnp.maximum(jnp.maximum(top_n, top_m), top_f)
            c_n = jnp.exp(top_n - top)
            c_m = jnp.exp(top_m - top)
            c_f = jnp.exp(top_f - top)
            under = (
                c_n * near[:, base + 32:base + 33]
                + c_m * middle[:, base + 32:base + 33]
                + c_f * far[:, base + 32:base + 33]
            )
            heads.append((c_n * near + c_m * middle + c_f * far) / under)
        lane = iota((256, 128), 1)
        lower = jnp.where(lane < 64, heads[0], heads[1])
        upper = jnp.where(lane < 64, heads[2], 0.0)
        return jnp.concatenate([lower, upper], axis=1).astype(BF)

    swaps = []
    for r, g in enumerate((right, opp, left)):
        ho_send[r] = merge(g)
        swap = rcopy(ho_send.at[r], ho_recv.at[h], hs.at[r], hr.at[r], me, g)
        swap.start()
        swaps.append(swap)
    ho_recv[h] = merge(h)
    weights_done(0)
    weights_last(1)
    for swap in swaps:
        swap.wait_recv()
    attended = jnp.zeros((SHARE, D), F32)
    for g in range(NH):
        attended = attended + dot(ho_recv[g, :, :192], outf[g]).astype(BF).astype(F32)
    residual = dense[pl.ds(pl.multiple_of(h * SHARE, SHARE), SHARE)] + attended
    normed_two = layer_norm(residual, mgain[...]).astype(BF)
    weights_pass(2)
    weights_done(1)
    weights_last(2)
    weights_done(2)

    def feed(g, total):
        hidden = dot(normed_two, upf[g])
        hidden = (0.5 * hidden * (1.0 + lax.erf(hidden * 0.7071067811865476))).astype(BF)
        return total + dot(hidden, downf[g]).astype(BF).astype(F32)

    o_ref[...] = (residual + lax.fori_loop(0, NH, feed, jnp.zeros((SHARE, D), F32))).astype(BF)

    all_first.wait_send()
    sent = send.at[pl.ds(WIN, (NS - 1) * WIN)]
    rcopy(sent, sent, s1_ss, s1_rs.at[0], me, right).wait_send()
    for ring in rings:
        for copy in ring:
            copy.wait_send()
    far_all.wait_send()
    far_s.wait_send()
    mid_z.wait_send()
    mid_s.wait_send()
    for swap in swaps:
        swap.wait_send()


def local(tile_features, kept_tiles, attn_gain, qkv_weight, out_weight, middle_head_offset,
          far_head_offset, mlp_gain, up_weight, down_weight):
    parts = qkv_weight.reshape(D, 3, HPD, HD)
    zero = jnp.zeros((D, HD), BF)
    columns = []
    for j in range(HPD):
        columns += [zero, parts[:, 0, j]] if v_first(j) else [parts[:, 0, j], zero]
    for j in range(HPD):
        columns += [parts[:, 2, j], parts[:, 1, j]] if v_first(j) else [parts[:, 1, j], parts[:, 2, j]]
    wqkv = jnp.concatenate(columns, axis=1)
    vmem = pl.BlockSpec(memory_space=pltpu.VMEM)
    smem = pl.BlockSpec(memory_space=pltpu.SMEM)
    hbm = pl.BlockSpec(memory_space=pl.ANY)
    dma = pltpu.SemaphoreType.DMA
    return pl.pallas_call(
        kernel,
        out_shape=jax.ShapeDtypeStruct((SHARE, D), BF),
        in_specs=[smem, smem, smem, vmem, vmem, vmem, vmem, vmem, hbm, hbm, hbm],
        out_specs=vmem,
        scratch_shapes=[
            pltpu.VMEM((NS * WIN, D), BF),
            pltpu.VMEM((4, NH, 128, D), BF),
            pltpu.VMEM((KD, 1), jnp.int32),
            pltpu.VMEM((KD, D), F32),
            pltpu.VMEM((KD, 384), BF),
            pltpu.VMEM((KD, 384), BF),
            pltpu.VMEM((256, 384), BF),
            pltpu.VMEM((64, 384), BF),
            pltpu.VMEM((2, 2, 256, 384), BF),
            pltpu.VMEM((2, 16, 64, 384), BF),
            pltpu.VMEM((HPD, KD, 128), F32),
            pltpu.VMEM((HPD, 256, 128), F32),
            pltpu.VMEM((HPD, 64, 128), F32),
            pltpu.VMEM((3, SHARE, 256), BF),
            pltpu.VMEM((NH, SHARE, 256), BF),
            pltpu.VMEM((8, 128), jnp.int32),
            pltpu.VMEM((NS, 8, 128), jnp.int32),
            pltpu.VMEM((NH, D, D), BF),
            pltpu.VMEM((NH, D, D), BF),
            pltpu.VMEM((NH, 192, D), BF),
            dma, dma, dma, dma((4,)), dma((4, 4)), dma((4, 4)), dma((3, 7)), dma((3, 7)), dma((3,)),
            dma((2,)), dma((2,)), dma((2,)), dma((2,)), dma((3,)), dma((3,)),
        ],
        compiler_params=pltpu.CompilerParams(
            collective_id=0, has_side_effects=True, vmem_limit_bytes=56 * 1024 * 1024
        ),
        cost_estimate=pl.CostEstimate(flops=12_000_000_000, bytes_accessed=20_000_000, transcendentals=5_000_000),
    )(
        kept_tiles, middle_head_offset, far_head_offset, kept_tiles.reshape(KD, 1), tile_features,
        attn_gain.reshape(1, D), wqkv, mlp_gain.reshape(1, D), up_weight, down_weight, out_weight,
    )


def solution(mesh):
    in_specs = (
        P(("seq", "head"), None),
        P("seq"),
        P(),
        P(None, None, "head"),
        P("head", None),
        P("head"),
        P("head"),
        P(),
        P(None, "head"),
        P("head", None),
    )
    out_specs = P(("seq", "head"), None)
    return jax.shard_map(local, mesh=mesh, in_specs=in_specs, out_specs=out_specs, check_vma=False)
```

```python
import functools

import jax
import jax.numpy as jnp
from jax import lax
from jax.experimental import pallas as pl
from jax.experimental.pallas import tpu as pltpu
from jax.sharding import PartitionSpec as P

NS = 32
NH = 4
ND = NS * NH
D = 768
KD = 1024
HD = 64
HPD = 3
WIN = 16
ROWS = 640
SHARE = KD // NH
EPS = 1e-05
NEG = -1e30
BF = jnp.bfloat16
F32 = jnp.float32


def dot(a, b):
    return lax.dot_general(a, b, (((1,), (0,)), ((), ())), preferred_element_type=F32)


def dot_nt(a, b):
    return lax.dot_general(a, b, (((1,), (1,)), ((), ())), preferred_element_type=F32)


def layer_norm(x, gain):
    centred = x - jnp.mean(x, axis=-1, keepdims=True)
    variance = jnp.mean(centred * centred, axis=-1, keepdims=True)
    return centred * lax.rsqrt(variance + EPS) * gain


def iota(shape, axis):
    return lax.broadcasted_iota(jnp.int32, shape, axis)


def v_first(head):
    return head != 1


def kernel(
    moff, foff, kept8, again6, mgain6, feat_in, qkv_in, up, down, outw,
    o_ref,
    feat, wraw, wqkv, send, recv, slot, dense, q, kv, qmid, qfar, normed, midkv, farkv, acc, accm, accf,
    ho_send, ho_recv, fk_send, fk_recv, upf, downf, outf,
    fk_ss, fk_rs, s1_ss, s1_rs, xs, xr, os, orr, bs, br, wl, ls, ms, mr, fs, fr, hs, hr,
):
    me = lax.axis_index("seq")
    h = lax.axis_index("head")
    right, left, opp = (h + 1) % NH, (h + 3) % NH, (h + 2) % NH
    core = me % 2
    chip = me // 2
    sib = me + 1 - 2 * core
    zbit = chip % 2
    zpart = me + 2 - 4 * zbit
    source = me * NH + h
    ypos, zpos = chip // 4, chip % 4
    a = ypos * (1 - core) + zpos * core
    b = zpos * (1 - core) + ypos * core
    a_next, a_prev, b_next, b_prev, b_opp = (a + 1) % 4, (a + 3) % 4, (b + 1) % 4, (b + 3) % 4, (b + 2) % 4

    def along(da, db):
        y = (ypos + (1 - core) * da + core * db) % 4
        z = (zpos + core * da + (1 - core) * db) % 4
        return (y * 4 + z) * 2 + core


    def rcopy(src, dst, ssem, rsem, seq, head):
        return pltpu.make_async_remote_copy(
            src_ref=src, dst_ref=dst, send_sem=ssem, recv_sem=rsem,
            device_id=(seq, head), device_id_type=pl.DeviceIdType.MESH,
        )

    feat_load = pltpu.make_async_copy(feat_in, feat, ls.at[0])
    feat_load.start()
    qkv_load = pltpu.make_async_copy(qkv_in, wraw, ls.at[1])
    qkv_load.start()
    again = jnp.concatenate([again6[k:k + 1] for k in range(6)], axis=1)
    mgain = jnp.concatenate([mgain6[k:k + 1] for k in range(6)], axis=1)

    barrier = pltpu.get_barrier_semaphore()

    def greet(i, c):
        pl.semaphore_signal(barrier, inc=1, device_id=((me + i) % NS, h), device_id_type=pl.DeviceIdType.MESH)
        return c

    lax.fori_loop(1, NS, greet, 0)
    for other in (right, left, opp):
        pl.semaphore_signal(barrier, inc=1, device_id=(me, other), device_id_type=pl.DeviceIdType.MESH)
    first = kept8[0:1, 0:1]
    fk_send[...] = jnp.broadcast_to(first, (8, 128))
    fk_recv[0] = fk_send[...]
    pl.semaphore_wait(barrier, NS - 1 + NH - 1)

    def send_first(i, c):
        rcopy(fk_send, fk_recv.at[(NS - i) % 4 * 8 + (NS - i) // 4], fk_ss, fk_rs, (me + i) % NS, h).start()
        return c

    lax.fori_loop(1, NS, send_first, 0)

    out_local = pltpu.make_async_copy(outw, outf.at[h], wl.at[2])
    lo = pl.multiple_of(core * 96, 16)
    own = pl.ds(lo, 96)
    out_mine = [
        rcopy(outw.at[own], outf.at[h, own], os.at[0], orr.at[0], me, right),
        rcopy(outw.at[own], outf.at[h, own], os.at[1], orr.at[1], me, left),
    ]
    at_l, at_r = pl.ds(lo, 48), pl.ds(pl.multiple_of(core * 96 + 48, 16), 48)
    out_ahead = [
        rcopy(outf.at[left, at_l], outf.at[left, at_l], os.at[2], orr.at[2], me, right),
        rcopy(outf.at[right, at_r], outf.at[right, at_r], os.at[3], orr.at[3], me, left),
    ]
    out_twin = [
        rcopy(outf.at[f, own], outf.at[f, own], os.at[4 + k], orr.at[4 + k], sib, h)
        for k, f in enumerate((left, right, opp))
    ]

    def eighth(at, skip, count):
        return pl.ds(pl.multiple_of(core * 384 + at * 96 + skip, 16), count)

    half = pl.ds(pl.multiple_of(core * 384, 16), 384)
    big_local, big_x1, big_x2, big_a1, big_a2, big_twin = [], [], [], [[], [], []], [[], [], []], [[], [], []]
    for w, (inp, full) in enumerate(((up, upf), (down, downf))):
        def same(f, rows, k, seq, head):
            return rcopy(full.at[f, rows], full.at[f, rows], bs.at[w, k], br.at[w, k], seq, head)

        big_local.append(pltpu.make_async_copy(inp, full.at[h], wl.at[w]))
        mine = eighth(a, 0, 96)
        for k, other in enumerate((right, left)):
            big_x1.append(rcopy(inp.at[mine], full.at[h, mine], bs.at[w, k], br.at[w, k], me, other))
        big_x2.append(same(left, eighth(a, 0, 48), 2, me, right))
        big_x2.append(same(right, eighth(a, 48, 48), 3, me, left))
        for k, f in enumerate((left, right, opp)):
            big_a1[k].append(same(f, mine, 4 + k, along(1, 0), h))
            big_a1[k].append(same(f, mine, 7 + k, along(3, 0), h))
            big_a2[k].append(same(f, eighth(a_prev, 0, 48), 10 + k, along(1, 0), h))
            big_a2[k].append(same(f, eighth(a_next, 48, 48), 13 + k, along(3, 0), h))
            big_twin[k].append(same(f, half, 16 + k, sib, h))

    def start(copies):
        for copy in copies:
            copy.start()
            drains.append(copy.wait_send)

    def arrived(copies):
        for copy in copies:
            copy.wait_recv()

    drains = [lambda: all_first.wait_send()]
    for copy in [out_local] + big_local:
        copy.start()
    start(out_mine)
    start(big_x1)

    for r in range(KD // 128):
        kc = jnp.broadcast_to(kept8[r:r + 1], (128, 128)).T
        sender = kc & (ND - 1)
        s_seq, s_head = lax.shift_right_arithmetic(sender, 2), sender & (NH - 1)
        within = lax.shift_right_arithmetic(kc, 7) - lax.shift_right_arithmetic(first - sender + (ND - 1), 7)
        rel = (me - s_seq + NS) & (NS - 1)
        slot[r * 128:(r + 1) * 128] = (
            (rel & 3) * 32 + s_head * 8 + lax.shift_right_arithmetic(rel, 2)
        ) * WIN + within

    all_first = rcopy(fk_recv.at[pl.ds(1, NS - 1)], fk_recv.at[pl.ds(1, NS - 1)], fk_ss, fk_rs, me, right)
    all_first.wait_recv()

    feat_load.wait()

    def send_windows(g):
        start = lax.shift_right_arithmetic(fk_recv[g * 8:g * 8 + 8] - source + (ND - 1), 7)
        start = jnp.concatenate([start, start], axis=1).reshape(128, 128)
        want = start + iota((128, 128), 0) % WIN - iota((128, 128), 1)
        pick = jnp.concatenate(
            [(want == t * 128).astype(F32).astype(BF) for t in range(ROWS // 128)], axis=1
        )
        send[g * 128:(g + 1) * 128] = dot(pick, feat[...]).astype(BF)

        def one(i, c):
            rcopy(
                send.at[pl.ds(pl.multiple_of(g * 128 + i * WIN, WIN), WIN)],
                recv.at[g, h, pl.ds(pl.multiple_of(i * WIN, WIN), WIN)],
                s1_ss, s1_rs.at[g], (me + 4 * i + g) % NS, h,
            ).start()
            return c

        lax.fori_loop(1 if g == 0 else 0, 8, one, 0)
        if g == 0:
            recv[0, h, 0:WIN] = send[0:WIN]

    sent = send.at[pl.ds(WIN, (NS - 1) * WIN)]
    drains.append(lambda: rcopy(sent, sent, s1_ss, s1_rs.at[0], me, right).wait_send())

    def arrive(g):
        lo = WIN if g == 0 else 0
        part = recv.at[g, h, pl.ds(lo, 128 - lo)]
        rcopy(part, part, s1_ss, s1_rs.at[g], me, right).wait_recv()

    rings = []
    for g in range(4):
        rings.append((
            rcopy(recv.at[g, h], recv.at[g, h], xs.at[g, 0], xr.at[g, 0], me, right),
            rcopy(recv.at[g, h], recv.at[g, h], xs.at[g, 1], xr.at[g, 1], me, left),
            rcopy(recv.at[g, left, pl.ds(0, 64)], recv.at[g, left, pl.ds(0, 64)], xs.at[g, 2], xr.at[g, 2], me, right),
            rcopy(recv.at[g, right, pl.ds(64, 64)], recv.at[g, right, pl.ds(64, 64)], xs.at[g, 3], xr.at[g, 3], me, left),
        ))

    def compact(g):
        rings[g][2].wait_recv()
        rings[g][3].wait_recv()

        def block(b, c):
            at = pl.ds(pl.multiple_of(b * 256, 256), 256)
            want = slot[at] - g * 512 - iota((256, 128), 1)
            pick = jnp.concatenate([(want == t * 128).astype(F32).astype(BF) for t in range(4)], axis=1)
            got = dot(pick, recv[g].reshape(512, D))
            if g == 0:
                dense[at] = got
            else:
                dense[at] = dense[at] + got
            return c

        lax.fori_loop(0, KD // 256, block, 0)

    def ring_pass(g):
        rings[g][0].wait_recv()
        rings[g][2].start()
        rings[g][1].wait_recv()
        rings[g][3].start()

    drains += [copy.wait_send for ring in rings for copy in ring]
    def ring_start(g):
        arrive(g)
        rings[g][0].start()
        rings[g][1].start()

    send_windows(0)
    send_windows(1)
    ring_start(0)
    send_windows(2)
    ring_start(1)
    send_windows(3)
    ring_pass(0)
    qkv_load.wait()
    for j in range(HPD):
        low, high = j * 128, j * 128 + 64
        rows = slice(j * 64, j * 64 + 64)
        at_q, at_0 = (high, low) if v_first(j) else (low, high)
        wqkv[at_0:at_0 + 64] = jnp.zeros((64, D), BF)
        wqkv[at_q:at_q + 64] = (wraw[0, rows].astype(F32) * 0.125).astype(BF)
        wqkv[384 + at_q:384 + at_q + 64] = wraw[1, rows]
        wqkv[384 + at_0:384 + at_0 + 64] = wraw[2, rows]
    ring_start(2)
    ring_pass(1)
    arrived(big_x1)
    start(big_a1[0] + big_a1[1])
    ring_start(3)
    ring_pass(2)
    compact(0)
    ring_pass(3)
    start(big_x2)
    arrived(out_mine)
    start(out_ahead + out_twin[:2])
    arrived(big_a1[0] + big_a1[1])
    start(big_a2[0] + big_a2[1])
    compact(1)
    compact(2)
    compact(3)

    def project_kv(blk, c):
        at = pl.ds(pl.multiple_of(blk * 256, 256), 256)
        block = layer_norm(dense[at], again).astype(BF)
        normed[at] = block
        kvb = dot_nt(block, wqkv[384:]).astype(BF)
        kv[at] = kvb
        at_m = pl.ds(pl.multiple_of(blk * 64, 64), 64)
        at_f = pl.ds(pl.multiple_of(blk * 16, 16), 16)
        for j in range(HPD):
            cols = slice(j * 128, (j + 1) * 128)
            sel = (iota((64, 256), 1) == iota((64, 256), 0) * 4 + moff[j]).astype(F32).astype(BF)
            midkv[core, zbit, at_m, cols] = dot(sel, kvb[:, cols]).astype(BF)
            sel = (iota((16, 256), 1) == iota((16, 256), 0) * 16 + foff[j]).astype(F32).astype(BF)
            farkv[core, b, a, at_f, cols] = dot(sel, kvb[:, cols]).astype(BF)
        return c

    lax.fori_loop(0, KD // 256, project_kv, 0)

    def far_copy(at, k, seq):
        return rcopy(farkv.at[at], farkv.at[at], fs.at[k], fr.at[k], seq, h)

    far_a1 = [far_copy((core, b, a), 0, along(1, 0)), far_copy((core, b, a), 1, along(3, 0))]
    far_a2 = [
        far_copy((core, b, a_prev, pl.ds(0, 32)), 2, along(1, 0)),
        far_copy((core, b, a_next, pl.ds(32, 32)), 3, along(3, 0)),
    ]
    far_b1 = [far_copy((core, b), 4, along(0, 1)), far_copy((core, b), 5, along(0, 3))]
    far_b2 = [
        far_copy((core, b_prev, pl.ds(0, 2)), 6, along(0, 1)),
        far_copy((core, b_next, pl.ds(2, 2)), 7, along(0, 3)),
    ]
    far_twin = [far_copy((core, at), 8 + k, sib) for k, at in enumerate((b, b_prev, b_next, b_opp))]
    mid_z = rcopy(midkv.at[core, zbit], midkv.at[core, zbit], ms.at[0], mr.at[0], zpart, h)
    mid_s = rcopy(midkv.at[core], midkv.at[core], ms.at[1], mr.at[1], sib, h)
    start(far_a1)
    start([mid_z])

    def project_q(blk, c):
        at = pl.ds(pl.multiple_of(blk * 256, 256), 256)
        qb = dot_nt(normed[at], wqkv[:384]).astype(BF)
        q[at] = qb
        at_m = pl.ds(pl.multiple_of(blk * 64, 64), 64)
        at_f = pl.ds(pl.multiple_of(blk * 16, 16), 16)
        for j in range(HPD):
            cols = slice(j * 128, (j + 1) * 128)
            sel = (iota((64, 256), 1) == iota((64, 256), 0) * 4 + moff[j]).astype(F32).astype(BF)
            qmid[at_m, cols] = dot(sel, qb[:, cols]).astype(BF)
            sel = (iota((16, 256), 1) == iota((16, 256), 0) * 16 + foff[j]).astype(F32).astype(BF)
            qfar[at_f, cols] = dot(sel, qb[:, cols]).astype(BF)
        return c

    lax.fori_loop(0, KD // 256, project_q, 0)
    arrived(far_a1)
    start(far_a2)

    def attend(qb, keys, j):
        scores = dot_nt(qb, keys)
        top = jnp.max(scores, axis=-1, keepdims=True)
        p = jnp.exp(scores - top)
        total = jnp.sum(p, axis=-1, keepdims=True)
        out = dot(p.astype(BF), keys)
        lane = iota(out.shape, 1)
        base = 64 if v_first(j) else 0
        out = jnp.where((lane >= base) & (lane < base + 32), top, out)
        return jnp.where((lane >= base + 32) & (lane < base + 64), total, out)

    def short(j, first_block):
        cols = slice(j * 128, (j + 1) * 128)

        def block(blk, c):
            at = pl.ds(pl.multiple_of(blk * 256, 256), 256)
            acc[j, at] = attend(q[at, cols], kv[:, cols], j)
            return c

        lax.fori_loop(first_block, first_block + 2, block, 0)

    short(0, 0)
    arrived(far_a2)
    start(far_b1 + far_twin[:1])
    arrived(big_x2)
    start(big_a1[2])
    arrived(big_a2[0] + big_a2[1])
    start(big_twin[0] + big_twin[1])
    short(0, 2)
    short(1, 0)
    arrived(far_b1)
    start(far_b2 + far_twin[1:3])
    short(1, 2)
    arrived([mid_z])
    start([mid_s])
    arrived(big_a1[2])
    start(big_a2[2])
    short(2, 0)
    arrived(far_b2)
    start(far_twin[3:])
    arrived(out_ahead)
    start(out_twin[2:])
    short(2, 2)
    arrived(big_a2[2])
    start(big_twin[2])
    arrived([mid_s])
    for j in range(HPD):
        cols = slice(j * 128, (j + 1) * 128)
        accm[j] = attend(qmid[:, cols], midkv[:, :, :, cols].reshape(KD, 128), j)
    arrived(far_twin)
    for j in range(HPD):
        cols = slice(j * 128, (j + 1) * 128)
        accf[j] = attend(qfar[:, cols], farkv[:, :, :, :, cols].reshape(2048, 128), j)

    def spread(one_hot, x):
        one = x.astype(BF)
        rest = x - one.astype(F32)
        two = rest.astype(BF)
        three = (rest - two.astype(F32)).astype(BF)
        return dot(one_hot, one) + dot(one_hot, two) + dot(one_hot, three)

    def merge(g):
        heads = []
        at = pl.ds(pl.multiple_of(g * 256, 256), 256)
        at_m = pl.ds(pl.multiple_of(g * 64, 64), 64)
        at_f = pl.ds(pl.multiple_of(g * 16, 16), 16)
        for j in range(HPD):
            base = 64 if v_first(j) else 0
            near = acc[j, at]
            hot_m = (iota((256, 64), 0) == iota((256, 64), 1) * 4 + moff[j]).astype(F32).astype(BF)
            hot_f = (iota((256, 16), 0) == iota((256, 16), 1) * 16 + foff[j]).astype(F32).astype(BF)
            middle = spread(hot_m, accm[j, at_m])
            far = spread(hot_f, accf[j, at_f])
            pos = iota((256, 1), 0)
            in_m = pos % 4 == moff[j]
            in_f = pos % 16 == foff[j]
            top_n = near[:, base:base + 1]
            top_m = jnp.where(in_m, middle[:, base:base + 1], NEG)
            top_f = jnp.where(in_f, far[:, base:base + 1], NEG)
            top = jnp.maximum(jnp.maximum(top_n, top_m), top_f)
            c_n = jnp.exp(top_n - top)
            c_m = jnp.exp(top_m - top)
            c_f = jnp.exp(top_f - top)
            under = (
                c_n * near[:, base + 32:base + 33]
                + c_m * middle[:, base + 32:base + 33]
                + c_f * far[:, base + 32:base + 33]
            )
            heads.append((c_n * near + c_m * middle + c_f * far) / under)
        lane = iota((256, 128), 1)
        lower = jnp.where(lane < 64, heads[0], heads[1])
        third = heads[2]
        upper = jnp.where(lane[:128] < 64, third[:128], pltpu.roll(third[128:], 64, 1))
        return lower.astype(BF), upper.astype(BF)

    swaps = []
    for r, g in enumerate((opp, right, left)):
        ho_send[r, :256], ho_send[r, 256:] = merge(g)
        swap = rcopy(ho_send.at[r], ho_recv.at[h], hs.at[r], hr.at[r], me, g)
        start([swap])
        swaps.append(swap)
    ho_recv[h, :256], ho_recv[h, 256:] = merge(h)
    out_local.wait()
    arrived(out_twin)
    arrived(swaps)
    attended = jnp.zeros((SHARE, D), F32)
    lane = iota((128, 128), 1)
    for g in range(NH):
        third = ho_recv[g, 256:]
        zero = jnp.zeros_like(third)
        third = jnp.concatenate([jnp.where(lane < 64, third, zero), jnp.where(lane < 64, zero, third)], axis=0)
        tail = outf[g, 128:]
        product = dot(ho_recv[g, :256], outf[g, :128]) + dot(third, jnp.concatenate([tail, tail], axis=0))
        attended = attended + product.astype(BF).astype(F32)
    residual = dense[pl.ds(pl.multiple_of(h * SHARE, SHARE), SHARE)] + attended
    normed_two = layer_norm(residual, mgain).astype(BF)
    for copy in big_local:
        copy.wait()
    arrived(big_twin[0] + big_twin[1] + big_twin[2])

    def feed(g, total):
        hidden = dot(normed_two, upf[g])
        hidden = (0.5 * hidden * (1.0 + lax.erf(hidden * 0.7071067811865476))).astype(BF)
        return total + dot(hidden, downf[g]).astype(BF).astype(F32)

    o_ref[...] = (residual + lax.fori_loop(0, NH, feed, jnp.zeros((SHARE, D), F32))).astype(BF)

    for drain in drains:
        drain()


def local(tile_features, kept_tiles, attn_gain, qkv_weight, out_weight, middle_head_offset,
          far_head_offset, mlp_gain, up_weight, down_weight):
    vmem = pl.BlockSpec(memory_space=pltpu.VMEM)
    smem = pl.BlockSpec(memory_space=pltpu.SMEM)
    hbm = pl.BlockSpec(memory_space=pl.ANY)
    dma = pltpu.SemaphoreType.DMA
    return pl.pallas_call(
        kernel,
        out_shape=jax.ShapeDtypeStruct((SHARE, D), BF),
        in_specs=[smem, smem, vmem, vmem, vmem, hbm, hbm, hbm, hbm, hbm],
        out_specs=vmem,
        scratch_shapes=[
            pltpu.VMEM((ROWS, D), BF),
            pltpu.VMEM((3, 192, D), BF),
            pltpu.VMEM((D, D), BF),
            pltpu.VMEM((NS * WIN, D), BF),
            pltpu.VMEM((4, NH, 128, D), BF),
            pltpu.VMEM((KD, 128), jnp.int32),
            pltpu.VMEM((KD, D), F32),
            pltpu.VMEM((KD, 384), BF),
            pltpu.VMEM((KD, 384), BF),
            pltpu.VMEM((256, 384), BF),
            pltpu.VMEM((64, 384), BF),
            pltpu.VMEM((KD, D), BF),
            pltpu.VMEM((2, 2, 256, 384), BF),
            pltpu.VMEM((2, 4, 4, 64, 384), BF),
            pltpu.VMEM((HPD, KD, 128), F32),
            pltpu.VMEM((HPD, 256, 128), F32),
            pltpu.VMEM((HPD, 64, 128), F32),
            pltpu.VMEM((3, 384, 128), BF),
            pltpu.VMEM((NH, 384, 128), BF),
            pltpu.VMEM((8, 128), jnp.int32),
            pltpu.VMEM((NS, 8, 128), jnp.int32),
            pltpu.VMEM((NH, D, D), BF),
            pltpu.VMEM((NH, D, D), BF),
            pltpu.VMEM((NH, 192, D), BF),
            dma, dma, dma, dma((4,)), dma((4, 4)), dma((4, 4)), dma((7,)), dma((7,)), dma((2, 19)), dma((2, 19)),
            dma((3,)), dma((2,)), dma((2,)), dma((2,)), dma((12,)), dma((12,)), dma((3,)), dma((3,)),
        ],
        compiler_params=pltpu.CompilerParams(
            collective_id=0, has_side_effects=True, vmem_limit_bytes=56 * 1024 * 1024
        ),
        cost_estimate=pl.CostEstimate(flops=12_000_000_000, bytes_accessed=20_000_000, transcendentals=5_000_000),
    )(
        middle_head_offset, far_head_offset, kept_tiles.reshape(8, 128), attn_gain.reshape(6, 128),
        mlp_gain.reshape(6, 128), tile_features, qkv_weight.transpose(1, 2, 0), up_weight, down_weight, out_weight,
    )


def solution(mesh):
    in_specs = (
        P(("seq", "head"), None),
        P("seq"),
        P(),
        P(None, None, "head"),
        P("head", None),
        P("head"),
        P("head"),
        P(),
        P(None, "head"),
        P("head", None),
    )
    out_specs = P(("seq", "head"), None)
    return jax.shard_map(local, mesh=mesh, in_specs=in_specs, out_specs=out_specs, check_vma=False)
```

```python
import functools

import jax
import jax.numpy as jnp
from jax import lax
from jax.experimental import pallas as pl
from jax.experimental.pallas import tpu as pltpu
from jax.sharding import PartitionSpec as P

NS = 32
NH = 4
ND = NS * NH
D = 768
KD = 1024
HD = 64
HPD = 3
WIN = 16
GROUPS = 8
PER = NS // GROUPS
GROWS = PER * WIN
ROWS = 640
SHARE = KD // NH
EPS = 1e-05
NEG = -1e30
CHIPS = (
    (0, 0), (0, 1), (0, 3), (1, 0), (3, 0), (1, 1), (1, 3), (3, 1),
    (3, 3), (0, 2), (2, 0), (1, 2), (2, 1), (2, 3), (3, 2), (2, 2),
)
PLACES = tuple((dy, dz, dc) for dy, dz in CHIPS for dc in (0, 1))
BF = jnp.bfloat16
F32 = jnp.float32


def dot(a, b):
    return lax.dot_general(a, b, (((1,), (0,)), ((), ())), preferred_element_type=F32)


def dot_nt(a, b):
    return lax.dot_general(a, b, (((1,), (1,)), ((), ())), preferred_element_type=F32)


def layer_norm(x, gain):
    centred = x - jnp.mean(x, axis=-1, keepdims=True)
    variance = jnp.mean(centred * centred, axis=-1, keepdims=True)
    return centred * lax.rsqrt(variance + EPS) * gain


def iota(shape, axis):
    return lax.broadcasted_iota(jnp.int32, shape, axis)


def v_first(head):
    return head != 1


def kernel(
    moff, foff, kept8, again6, mgain6, feat_in, qkv_in, up, down, outw,
    o_ref,
    feat, wraw, wqkv, send, recv, slot, dense, q, kv, qmid, qfar, normed, nfar, midkv, farkv, acc, accm, accf,
    ho_send, ho_recv, fk_send, fk_recv, upf, downf, outf,
    fk_ss, fk_rs, s1_ss, s1_rs, xs, xr, os, orr, bs, br, wl, ls, ms, mr, fs, fr, hs, hr,
):
    me = lax.axis_index("seq")
    h = lax.axis_index("head")
    right, left, opp = (h + 1) % NH, (h + 3) % NH, (h + 2) % NH
    core = me % 2
    chip = me // 2
    sib = me + 1 - 2 * core
    zbit = chip % 2
    zpart = me + 2 - 4 * zbit
    source = me * NH + h
    ypos, zpos = chip // 4, chip % 4
    a = ypos * (1 - core) + zpos * core
    b = zpos * (1 - core) + ypos * core
    a_next, a_prev, b_next, b_prev, b_opp = (a + 1) % 4, (a + 3) % 4, (b + 1) % 4, (b + 3) % 4, (b + 2) % 4

    def along(da, db):
        y = (ypos + (1 - core) * da + core * db) % 4
        z = (zpos + core * da + (1 - core) * db) % 4
        return (y * 4 + z) * 2 + core


    def offset(n, sign):
        dy, dz, dc = PLACES[n]
        return ((ypos + sign * dy) % 4 * 4 + (zpos + sign * dz) % 4) * 2 + (core + dc) % 2

    def rcopy(src, dst, ssem, rsem, seq, head):
        return pltpu.make_async_remote_copy(
            src_ref=src, dst_ref=dst, send_sem=ssem, recv_sem=rsem,
            device_id=(seq, head), device_id_type=pl.DeviceIdType.MESH,
        )

    feat_load = pltpu.make_async_copy(feat_in, feat, ls.at[0])
    feat_load.start()
    qkv_load = pltpu.make_async_copy(qkv_in, wraw, ls.at[1])
    qkv_load.start()
    again = jnp.concatenate([again6[k:k + 1] for k in range(6)], axis=1)
    mgain = jnp.concatenate([mgain6[k:k + 1] for k in range(6)], axis=1)

    barrier = pltpu.get_barrier_semaphore()

    for n in range(1, NS):
        pl.semaphore_signal(barrier, inc=1, device_id=(offset(n, 1), h), device_id_type=pl.DeviceIdType.MESH)
    for other in (right, left, opp):
        pl.semaphore_signal(barrier, inc=1, device_id=(me, other), device_id_type=pl.DeviceIdType.MESH)
    first = kept8[0:1, 0:1]
    fk_send[...] = jnp.broadcast_to(first, (8, 128))
    fk_recv[0] = fk_send[...]
    pl.semaphore_wait(barrier, NS - 1 + NH - 1)

    for n in range(1, NS):
        rcopy(fk_send, fk_recv.at[n], fk_ss, fk_rs.at[n // PER], offset(n, 1), h).start()

    out_local = pltpu.make_async_copy(outw, outf.at[h], wl.at[2])
    lo = pl.multiple_of(core * 96, 16)
    own = pl.ds(lo, 96)
    out_mine = [
        rcopy(outw.at[own], outf.at[h, own], os.at[0], orr.at[0], me, right),
        rcopy(outw.at[own], outf.at[h, own], os.at[1], orr.at[1], me, left),
    ]
    at_l, at_r = pl.ds(lo, 48), pl.ds(pl.multiple_of(core * 96 + 48, 16), 48)
    out_ahead = [
        rcopy(outf.at[left, at_l], outf.at[left, at_l], os.at[2], orr.at[2], me, right),
        rcopy(outf.at[right, at_r], outf.at[right, at_r], os.at[3], orr.at[3], me, left),
    ]
    out_twin = [
        rcopy(outf.at[f, own], outf.at[f, own], os.at[4 + k], orr.at[4 + k], sib, h)
        for k, f in enumerate((left, right, opp))
    ]

    def eighth(at, skip, count):
        return pl.ds(pl.multiple_of(core * 384 + at * 96 + skip, 16), count)

    half = pl.ds(pl.multiple_of(core * 384, 16), 384)
    big_local, big_x1, big_x2, big_a1, big_a2, big_twin = [], [], [], [[], [], []], [[], [], []], [[], [], []]
    for w, (inp, full) in enumerate(((up, upf), (down, downf))):
        def same(f, rows, k, seq, head):
            return rcopy(full.at[f, rows], full.at[f, rows], bs.at[w, k], br.at[w, k], seq, head)

        big_local.append(pltpu.make_async_copy(inp, full.at[h], wl.at[w]))
        mine = eighth(a, 0, 96)
        for k, other in enumerate((right, left)):
            big_x1.append(rcopy(inp.at[mine], full.at[h, mine], bs.at[w, k], br.at[w, k], me, other))
        big_x2.append(same(left, eighth(a, 0, 48), 2, me, right))
        big_x2.append(same(right, eighth(a, 48, 48), 3, me, left))
        for k, f in enumerate((left, right, opp)):
            big_a1[k].append(same(f, mine, 4 + k, along(1, 0), h))
            big_a1[k].append(same(f, mine, 7 + k, along(3, 0), h))
            big_a2[k].append(same(f, eighth(a_prev, 0, 48), 10 + k, along(1, 0), h))
            big_a2[k].append(same(f, eighth(a_next, 48, 48), 13 + k, along(3, 0), h))
            big_twin[k].append(same(f, half, 16 + k, sib, h))

    def start(copies):
        for copy in copies:
            copy.start()
            drains.append(copy.wait_send)

    def arrived(copies):
        for copy in copies:
            copy.wait_recv()

    all_first = fk_recv.at[pl.ds(1, NS - 1)]
    drains = [lambda: rcopy(all_first, all_first, fk_ss, fk_rs.at[0], me, right).wait_send()]
    for copy in [out_local] + big_local:
        copy.start()
    start(big_x1)

    for r in range(KD // 128):
        kc = jnp.broadcast_to(kept8[r:r + 1], (128, 128)).T
        sender = kc & (ND - 1)
        s_seq, s_head = lax.shift_right_arithmetic(sender, 2), sender & (NH - 1)
        within = lax.shift_right_arithmetic(kc, 7) - lax.shift_right_arithmetic(first - sender + (ND - 1), 7)
        way = (lax.shift_right_arithmetic(s_seq, 3) - ypos) & 3
        way = way * 4 + ((lax.shift_right_arithmetic(s_seq, 1) - zpos) & 3)
        words = [sum(CHIPS.index(divmod(8 * half + k, 4)) << (4 * k) for k in range(7)) for half in (0, 1)]
        last = [CHIPS.index(divmod(8 * half + 7, 4)) for half in (0, 1)]
        place = lax.shift_right_arithmetic(jnp.where(way < 8, words[0], words[1]), (way & 7) * 4) & 15
        place = jnp.where((way & 7) == 7, jnp.where(way < 8, last[0], last[1]), place)
        rel = place * 2 + ((s_seq + core) & 1)
        slot[r * 128:(r + 1) * 128] = (
            lax.shift_right_arithmetic(rel, 2) * (PER * NH) + s_head * PER + (rel & (PER - 1))
        ) * WIN + within

    feat_load.wait()

    def send_windows(g):
        lo = 1 if g == 0 else 0
        firsts = fk_recv.at[pl.ds(g * PER + lo, PER - lo)]
        rcopy(firsts, firsts, fk_ss, fk_rs.at[g], me, right).wait_recv()
        start = lax.shift_right_arithmetic(fk_recv[g * PER:(g + 1) * PER] - source + (ND - 1), 7)
        start = jnp.concatenate([start, start], axis=1).reshape(GROWS, 128)
        want = start + iota((GROWS, 128), 0) % WIN - iota((GROWS, 128), 1)
        pick = jnp.concatenate(
            [(want == t * 128).astype(F32).astype(BF) for t in range(ROWS // 128)], axis=1
        )
        send[g * GROWS:(g + 1) * GROWS] = dot(pick, feat[...]).astype(BF)
        for i in range(lo, PER):
            rcopy(
                send.at[pl.ds(g * GROWS + i * WIN, WIN)], recv.at[g, h, pl.ds(i * WIN, WIN)],
                s1_ss, s1_rs.at[g], offset(g * PER + i, -1), h,
            ).start()
        if g == 0:
            recv[0, h, 0:WIN] = send[0:WIN]

    sent = send.at[pl.ds(WIN, (NS - 1) * WIN)]
    drains.append(lambda: rcopy(sent, sent, s1_ss, s1_rs.at[0], me, right).wait_send())

    def arrive(g):
        lo = WIN if g == 0 else 0
        part = recv.at[g, h, pl.ds(lo, GROWS - lo)]
        rcopy(part, part, s1_ss, s1_rs.at[g], me, right).wait_recv()

    rings = []
    for g in range(GROUPS):
        rings.append((
            rcopy(recv.at[g, h], recv.at[g, h], xs.at[g, 0], xr.at[g, 0], me, right),
            rcopy(recv.at[g, h], recv.at[g, h], xs.at[g, 1], xr.at[g, 1], me, left),
            rcopy(recv.at[g, left, pl.ds(0, GROWS // 2)], recv.at[g, left, pl.ds(0, GROWS // 2)], xs.at[g, 2], xr.at[g, 2], me, right),
            rcopy(recv.at[g, right, pl.ds(GROWS // 2, GROWS // 2)], recv.at[g, right, pl.ds(GROWS // 2, GROWS // 2)], xs.at[g, 3], xr.at[g, 3], me, left),
        ))

    def compact(g):
        for k in (2 * g, 2 * g + 1):
            rings[k][2].wait_recv()
            rings[k][3].wait_recv()

        def block(b, c):
            at = pl.ds(pl.multiple_of(b * 256, 256), 256)
            want = slot[at] - g * 512 - iota((256, 128), 1)
            pick = jnp.concatenate([(want == t * 128).astype(F32).astype(BF) for t in range(4)], axis=1)
            got = dot(pick, recv[2 * g:2 * g + 2].reshape(512, D))
            if g == 0:
                dense[at] = got
            else:
                dense[at] = dense[at] + got
            return c

        lax.fori_loop(0, KD // 256, block, 0)

    def ring_pass(g):
        rings[g][0].wait_recv()
        rings[g][2].start()
        rings[g][1].wait_recv()
        rings[g][3].start()

    drains += [copy.wait_send for ring in rings for copy in ring]
    def ring_start(g):
        arrive(g)
        rings[g][0].start()
        rings[g][1].start()

    send_windows(0)
    send_windows(1)
    ring_start(0)
    send_windows(2)
    ring_start(1)
    send_windows(3)
    send_windows(4)
    ring_pass(0)
    ring_start(2)
    send_windows(5)
    send_windows(6)
    ring_pass(1)
    ring_start(3)
    send_windows(7)
    ring_pass(2)
    ring_start(4)
    arrived(big_x1)
    start(big_a1[0] + big_a1[1])
    qkv_load.wait()
    for j in range(HPD):
        low, high = j * 128, j * 128 + 64
        rows = slice(j * 64, j * 64 + 64)
        at_q, at_0 = (high, low) if v_first(j) else (low, high)
        wqkv[at_0:at_0 + 64] = jnp.zeros((64, D), BF)
        wqkv[at_q:at_q + 64] = (wraw[0, rows].astype(F32) * 0.125).astype(BF)
        wqkv[384 + at_q:384 + at_q + 64] = wraw[1, rows]
        wqkv[384 + at_0:384 + at_0 + 64] = wraw[2, rows]
    ring_pass(3)
    ring_start(5)
    ring_pass(4)
    ring_start(6)
    ring_pass(5)
    ring_start(7)
    compact(0)
    arrived(big_a1[0] + big_a1[1])
    start(big_a2[0] + big_a2[1])
    ring_pass(6)
    compact(1)
    ring_pass(7)
    start(big_x2)
    start(out_mine)
    arrived(big_a2[0] + big_a2[1])
    start(big_twin[0] + big_twin[1])
    compact(2)
    compact(3)

    def norm(blk, c):
        block = layer_norm(dense[pl.ds(pl.multiple_of(blk * 256, 256), 256)], again).astype(BF)
        normed[pl.ds(pl.multiple_of(blk * 256, 256), 256)] = block
        row = iota((48, 256), 0)
        which = jnp.where(row < 16, foff[0], jnp.where(row < 32, foff[1], foff[2]))
        sel = (iota((48, 256), 1) == (row & 15) * 16 + which).astype(F32).astype(BF)
        rows = dot(sel, block).astype(BF)
        for j in range(HPD):
            nfar[j, pl.ds(pl.multiple_of(blk * 16, 16), 16)] = rows[j * 16:(j + 1) * 16]
        return c

    lax.fori_loop(0, KD // 256, norm, 0)
    for j in range(HPD):
        cols = slice(j * 128, (j + 1) * 128)
        farkv[core, b, a, :, cols] = dot_nt(nfar[j], wqkv[384 + j * 128:512 + j * 128]).astype(BF)

    def far_copy(at, k, seq):
        return rcopy(farkv.at[at], farkv.at[at], fs.at[k], fr.at[k], seq, h)

    a_opp = (a + 2) % 4
    spots = (a, a_prev, a_next, a_opp)
    far_a1 = [far_copy((core, b, a), 0, along(1, 0)), far_copy((core, b, a), 1, along(3, 0))]
    far_a2 = [
        far_copy((core, b, a_prev, pl.ds(0, 32)), 2, along(1, 0)),
        far_copy((core, b, a_next, pl.ds(32, 32)), 3, along(3, 0)),
    ]
    far_b1 = [
        [far_copy((core, b, x), 4 + 2 * k, along(0, 1)), far_copy((core, b, x), 5 + 2 * k, along(0, 3))]
        for k, x in enumerate(spots)
    ]
    far_b2 = [
        [
            far_copy((core, b_prev, x, pl.ds(0, 32)), 12 + 2 * k, along(0, 1)),
            far_copy((core, b_next, x, pl.ds(32, 32)), 13 + 2 * k, along(0, 3)),
        ]
        for k, x in enumerate(spots)
    ]
    far_twin = [far_copy((core, at), 20 + k, sib) for k, at in enumerate((b, b_prev, b_next, b_opp))]
    mid_z = rcopy(midkv.at[core, zbit], midkv.at[core, zbit], ms.at[0], mr.at[0], zpart, h)
    mid_s = rcopy(midkv.at[core], midkv.at[core], ms.at[1], mr.at[1], sib, h)
    start(far_a1 + far_b1[0])

    def project_kv(blk, c):
        at = pl.ds(pl.multiple_of(blk * 256, 256), 256)
        kvb = dot_nt(normed[at], wqkv[384:]).astype(BF)
        kv[at] = kvb
        at_m = pl.ds(pl.multiple_of(blk * 64, 64), 64)
        for j in range(HPD):
            cols = slice(j * 128, (j + 1) * 128)
            sel = (iota((64, 256), 1) == iota((64, 256), 0) * 4 + moff[j]).astype(F32).astype(BF)
            midkv[core, zbit, at_m, cols] = dot(sel, kvb[:, cols]).astype(BF)
        return c

    lax.fori_loop(0, KD // 256, project_kv, 0)
    start([mid_z])
    arrived(far_a1)
    start(far_a2 + far_b1[1] + far_b1[2])

    def project_q(blk, c):
        at = pl.ds(pl.multiple_of(blk * 256, 256), 256)
        qb = dot_nt(normed[at], wqkv[:384]).astype(BF)
        q[at] = qb
        at_m = pl.ds(pl.multiple_of(blk * 64, 64), 64)
        for j in range(HPD):
            cols = slice(j * 128, (j + 1) * 128)
            sel = (iota((64, 256), 1) == iota((64, 256), 0) * 4 + moff[j]).astype(F32).astype(BF)
            qmid[at_m, cols] = dot(sel, qb[:, cols]).astype(BF)
        return c

    lax.fori_loop(0, KD // 256, project_q, 0)
    for j in range(HPD):
        cols = slice(j * 128, (j + 1) * 128)
        qfar[:, cols] = dot_nt(nfar[j], wqkv[j * 128:(j + 1) * 128]).astype(BF)
    arrived(far_a2 + far_b1[0])
    start(far_b1[3] + far_b2[0] + far_twin[:1])

    def attend(qb, keys, j):
        scores = dot_nt(qb, keys)
        top = jnp.max(scores, axis=-1, keepdims=True)
        p = jnp.exp(scores - top)
        total = jnp.sum(p, axis=-1, keepdims=True)
        out = dot(p.astype(BF), keys)
        lane = iota(out.shape, 1)
        base = 64 if v_first(j) else 0
        out = jnp.where((lane >= base) & (lane < base + 32), top, out)
        return jnp.where((lane >= base + 32) & (lane < base + 64), total, out)

    def short(j, first_block):
        cols = slice(j * 128, (j + 1) * 128)

        def block(blk, c):
            at = pl.ds(pl.multiple_of(blk * 256, 256), 256)
            acc[j, at] = attend(q[at, cols], kv[:, cols], j)
            return c

        lax.fori_loop(first_block, first_block + 2, block, 0)

    arrived(out_mine)
    start(out_ahead + out_twin[:2])
    short(0, 0)
    short(0, 2)
    arrived(far_b1[1] + far_b1[2])
    start(far_b2[1] + far_b2[2])
    short(1, 0)
    arrived(far_b1[3])
    start(far_b2[3] + far_twin[1:3])
    short(1, 2)
    arrived([mid_z])
    start([mid_s])
    arrived(out_ahead)
    start(out_twin[2:])
    short(2, 0)
    for k in range(4):
        arrived(far_b2[k])
    start(far_twin[3:])
    arrived(big_x2)
    start(big_a1[2])
    short(2, 2)
    arrived([mid_s])
    for j in range(HPD):
        cols = slice(j * 128, (j + 1) * 128)
        accm[j] = attend(qmid[:, cols], midkv[:, :, :, cols].reshape(KD, 128), j)
    arrived(far_twin)
    for j in range(HPD):
        cols = slice(j * 128, (j + 1) * 128)
        accf[j] = attend(qfar[:, cols], farkv[:, :, :, :, cols].reshape(2048, 128), j)

    arrived(big_a1[2])
    start(big_a2[2])
    def spread(one_hot, x):
        one = x.astype(BF)
        rest = x - one.astype(F32)
        two = rest.astype(BF)
        three = (rest - two.astype(F32)).astype(BF)
        return dot(one_hot, one) + dot(one_hot, two) + dot(one_hot, three)

    def merge(g):
        heads = []
        at = pl.ds(pl.multiple_of(g * 256, 256), 256)
        at_m = pl.ds(pl.multiple_of(g * 64, 64), 64)
        at_f = pl.ds(pl.multiple_of(g * 16, 16), 16)
        for j in range(HPD):
            base = 64 if v_first(j) else 0
            near = acc[j, at]
            hot_m = (iota((256, 64), 0) == iota((256, 64), 1) * 4 + moff[j]).astype(F32).astype(BF)
            hot_f = (iota((256, 16), 0) == iota((256, 16), 1) * 16 + foff[j]).astype(F32).astype(BF)
            middle = spread(hot_m, accm[j, at_m])
            far = spread(hot_f, accf[j, at_f])
            pos = iota((256, 1), 0)
            in_m = pos % 4 == moff[j]
            in_f = pos % 16 == foff[j]
            top_n = near[:, base:base + 1]
            top_m = jnp.where(in_m, middle[:, base:base + 1], NEG)
            top_f = jnp.where(in_f, far[:, base:base + 1], NEG)
            top = jnp.maximum(jnp.maximum(top_n, top_m), top_f)
            c_n = jnp.exp(top_n - top)
            c_m = jnp.exp(top_m - top)
            c_f = jnp.exp(top_f - top)
            under = (
                c_n * near[:, base + 32:base + 33]
                + c_m * middle[:, base + 32:base + 33]
                + c_f * far[:, base + 32:base + 33]
            )
            heads.append((c_n * near + c_m * middle + c_f * far) / under)
        lane = iota((256, 128), 1)
        lower = jnp.where(lane < 64, heads[0], heads[1])
        third = heads[2]
        upper = jnp.where(lane[:128] < 64, third[:128], pltpu.roll(third[128:], 64, 1))
        return lower.astype(BF), upper.astype(BF)

    swaps = []
    for r, g in enumerate((opp, right, left)):
        ho_send[r, :256], ho_send[r, 256:] = merge(g)
        swap = rcopy(ho_send.at[r], ho_recv.at[h], hs.at[r], hr.at[r], me, g)
        start([swap])
        swaps.append(swap)
    ho_recv[h, :256], ho_recv[h, 256:] = merge(h)
    arrived(big_a2[2])
    start(big_twin[2])
    out_local.wait()
    arrived(out_twin)
    arrived(swaps)
    attended = jnp.zeros((SHARE, D), F32)
    lane = iota((128, 128), 1)
    for g in range(NH):
        third = ho_recv[g, 256:]
        zero = jnp.zeros_like(third)
        third = jnp.concatenate([jnp.where(lane < 64, third, zero), jnp.where(lane < 64, zero, third)], axis=0)
        tail = outf[g, 128:]
        product = dot(ho_recv[g, :256], outf[g, :128]) + dot(third, jnp.concatenate([tail, tail], axis=0))
        attended = attended + product.astype(BF).astype(F32)
    residual = dense[pl.ds(pl.multiple_of(h * SHARE, SHARE), SHARE)] + attended
    normed_two = layer_norm(residual, mgain).astype(BF)
    for copy in big_local:
        copy.wait()
    arrived(big_twin[0] + big_twin[1] + big_twin[2])

    total = residual
    for g in range(NH):
        hidden = dot(normed_two, upf[g])
        hidden = (0.5 * hidden * (1.0 + lax.erf(hidden * 0.7071067811865476))).astype(BF)
        total = total + dot(hidden, downf[g]).astype(BF).astype(F32)
    o_ref[...] = total.astype(BF)

    for drain in drains:
        drain()


def local(tile_features, kept_tiles, attn_gain, qkv_weight, out_weight, middle_head_offset,
          far_head_offset, mlp_gain, up_weight, down_weight):
    vmem = pl.BlockSpec(memory_space=pltpu.VMEM)
    smem = pl.BlockSpec(memory_space=pltpu.SMEM)
    hbm = pl.BlockSpec(memory_space=pl.ANY)
    dma = pltpu.SemaphoreType.DMA
    return pl.pallas_call(
        kernel,
        out_shape=jax.ShapeDtypeStruct((SHARE, D), BF),
        in_specs=[smem, smem, vmem, vmem, vmem, hbm, hbm, hbm, hbm, hbm],
        out_specs=vmem,
        scratch_shapes=[
            pltpu.VMEM((ROWS, D), BF),
            pltpu.VMEM((3, 192, D), BF),
            pltpu.VMEM((D, D), BF),
            pltpu.VMEM((NS * WIN, D), BF),
            pltpu.VMEM((GROUPS, NH, GROWS, D), BF),
            pltpu.VMEM((KD, 128), jnp.int32),
            pltpu.VMEM((KD, D), F32),
            pltpu.VMEM((KD, 384), BF),
            pltpu.VMEM((KD, 384), BF),
            pltpu.VMEM((256, 384), BF),
            pltpu.VMEM((64, 384), BF),
            pltpu.VMEM((KD, D), BF),
            pltpu.VMEM((HPD, 64, D), BF),
            pltpu.VMEM((2, 2, 256, 384), BF),
            pltpu.VMEM((2, 4, 4, 64, 384), BF),
            pltpu.VMEM((HPD, KD, 128), F32),
            pltpu.VMEM((HPD, 256, 128), F32),
            pltpu.VMEM((HPD, 64, 128), F32),
            pltpu.VMEM((3, 384, 128), BF),
            pltpu.VMEM((NH, 384, 128), BF),
            pltpu.VMEM((8, 128), jnp.int32),
            pltpu.VMEM((NS, 8, 128), jnp.int32),
            pltpu.VMEM((NH, D, D), BF),
            pltpu.VMEM((NH, D, D), BF),
            pltpu.VMEM((NH, 192, D), BF),
            dma, dma((GROUPS,)), dma, dma((GROUPS,)), dma((GROUPS, 4)), dma((GROUPS, 4)), dma((7,)), dma((7,)), dma((2, 19)), dma((2, 19)),
            dma((3,)), dma((2,)), dma((2,)), dma((2,)), dma((24,)), dma((24,)), dma((3,)), dma((3,)),
        ],
        compiler_params=pltpu.CompilerParams(
            collective_id=0, has_side_effects=True, vmem_limit_bytes=56 * 1024 * 1024
        ),
        cost_estimate=pl.CostEstimate(flops=12_000_000_000, bytes_accessed=20_000_000, transcendentals=5_000_000),
    )(
        middle_head_offset, far_head_offset, kept_tiles.reshape(8, 128), attn_gain.reshape(6, 128),
        mlp_gain.reshape(6, 128), tile_features, qkv_weight.transpose(1, 2, 0), up_weight, down_weight, out_weight,
    )


def solution(mesh):
    in_specs = (
        P(("seq", "head"), None),
        P("seq"),
        P(),
        P(None, None, "head"),
        P("head", None),
        P("head"),
        P("head"),
        P(),
        P(None, "head"),
        P("head", None),
    )
    out_specs = P(("seq", "head"), None)
    return jax.shard_map(local, mesh=mesh, in_specs=in_specs, out_specs=out_specs, check_vma=False)
```

```python
import functools

import jax
import jax.numpy as jnp
from jax import lax
from jax.experimental import pallas as pl
from jax.experimental.pallas import tpu as pltpu
from jax.sharding import PartitionSpec as P

NS = 32
NH = 4
ND = NS * NH
D = 768
KD = 1024
HD = 64
HPD = 3
WIN = 16
GROUPS = 8
PER = NS // GROUPS
GROWS = PER * WIN
ROWS = 640
SHARE = KD // NH
EPS = 1e-05
NEG = -1e30
CHIPS = (
    (0, 0), (0, 1), (0, 3), (1, 0), (3, 0), (1, 1), (1, 3), (3, 1),
    (3, 3), (0, 2), (2, 0), (1, 2), (2, 1), (2, 3), (3, 2), (2, 2),
)
PLACES = tuple((dy, dz, dc) for dy, dz in CHIPS for dc in (0, 1))
BF = jnp.bfloat16
F32 = jnp.float32


def dot(a, b):
    return lax.dot_general(a, b, (((1,), (0,)), ((), ())), preferred_element_type=F32)


def dot_nt(a, b):
    return lax.dot_general(a, b, (((1,), (1,)), ((), ())), preferred_element_type=F32)


def layer_norm(x, gain):
    centred = x - jnp.mean(x, axis=-1, keepdims=True)
    variance = jnp.mean(centred * centred, axis=-1, keepdims=True)
    return centred * lax.rsqrt(variance + EPS) * gain


def iota(shape, axis):
    return lax.broadcasted_iota(jnp.int32, shape, axis)


def v_first(head):
    return head != 1


def kernel(
    moff, foff, kept8, again6, mgain6, feat_in, qkv_in, up, down, outw,
    o_ref,
    feat, wraw, wqkv, wturn, send, recv, slot, dense, q, kv, qmid, qfar, normed, nfar, midkv, farkv, acc, accm, accf,
    ho_send, ho_recv, fk_send, fk_recv, upf, downf, outf,
    fk_ss, fk_rs, s1_ss, s1_rs, xs, xr, os, orr, bs, br, wl, ls, ms, mr, fs, fr, hs, hr,
):
    me = lax.axis_index("seq")
    h = lax.axis_index("head")
    right, left, opp = (h + 1) % NH, (h + 3) % NH, (h + 2) % NH
    core = me % 2
    chip = me // 2
    sib = me + 1 - 2 * core
    zbit = chip % 2
    zpart = me + 2 - 4 * zbit
    source = me * NH + h
    ypos, zpos = chip // 4, chip % 4
    a = ypos * (1 - core) + zpos * core
    b = zpos * (1 - core) + ypos * core
    a_next, a_prev, b_next, b_prev, b_opp = (a + 1) % 4, (a + 3) % 4, (b + 1) % 4, (b + 3) % 4, (b + 2) % 4

    def along(da, db):
        y = (ypos + (1 - core) * da + core * db) % 4
        z = (zpos + core * da + (1 - core) * db) % 4
        return (y * 4 + z) * 2 + core


    y_next, y_prev, z_next, z_prev = (ypos + 1) % 4, (ypos + 3) % 4, (zpos + 1) % 4, (zpos + 3) % 4

    def across(dy, dz):
        return ((ypos + dy) % 4 * 4 + (zpos + dz) % 4) * 2 + core

    def offset(n, sign):
        dy, dz, dc = PLACES[n]
        return ((ypos + sign * dy) % 4 * 4 + (zpos + sign * dz) % 4) * 2 + (core + dc) % 2

    def rcopy(src, dst, ssem, rsem, seq, head):
        return pltpu.make_async_remote_copy(
            src_ref=src, dst_ref=dst, send_sem=ssem, recv_sem=rsem,
            device_id=(seq, head), device_id_type=pl.DeviceIdType.MESH,
        )

    feat_load = pltpu.make_async_copy(feat_in, feat, ls.at[0])
    feat_load.start()
    qkv_load = pltpu.make_async_copy(qkv_in, wraw, ls.at[1])
    qkv_load.start()
    again = jnp.concatenate([again6[k:k + 1] for k in range(6)], axis=1)
    mgain = jnp.concatenate([mgain6[k:k + 1] for k in range(6)], axis=1)

    barrier = pltpu.get_barrier_semaphore()

    for n in range(1, NS):
        pl.semaphore_signal(barrier, inc=1, device_id=(offset(n, 1), h), device_id_type=pl.DeviceIdType.MESH)
    for other in (right, left, opp):
        pl.semaphore_signal(barrier, inc=1, device_id=(me, other), device_id_type=pl.DeviceIdType.MESH)
    first = kept8[0:1, 0:1]
    fk_send[...] = jnp.broadcast_to(first, (8, 128))
    fk_recv[0] = fk_send[...]
    pl.semaphore_wait(barrier, NS - 1 + NH - 1)

    for n in range(1, NS):
        rcopy(fk_send, fk_recv.at[n], fk_ss, fk_rs.at[n // PER], offset(n, 1), h).start()

    out_local = pltpu.make_async_copy(outw, outf.at[h], wl.at[2])
    lo = pl.multiple_of(core * 96, 16)
    own = pl.ds(lo, 96)
    out_mine = [
        rcopy(outw.at[own], outf.at[h, own], os.at[0], orr.at[0], me, right),
        rcopy(outw.at[own], outf.at[h, own], os.at[1], orr.at[1], me, left),
    ]
    at_l, at_r = pl.ds(lo, 48), pl.ds(pl.multiple_of(core * 96 + 48, 16), 48)
    out_ahead = [
        rcopy(outf.at[left, at_l], outf.at[left, at_l], os.at[2], orr.at[2], me, right),
        rcopy(outf.at[right, at_r], outf.at[right, at_r], os.at[3], orr.at[3], me, left),
    ]
    out_twin = [
        rcopy(outf.at[f, own], outf.at[f, own], os.at[4 + k], orr.at[4 + k], sib, h)
        for k, f in enumerate((left, right, opp))
    ]

    def eighth(at, skip, count):
        return pl.ds(pl.multiple_of(core * 384 + at * 96 + skip, 16), count)

    half = pl.ds(pl.multiple_of(core * 384, 16), 384)
    big_local, big_x1, big_x2, big_a1, big_a2, big_twin = [], [], [], [[], [], []], [[], [], []], [[], [], []]
    for w, (inp, full) in enumerate(((up, upf), (down, downf))):
        def same(f, rows, k, seq, head):
            return rcopy(full.at[f, rows], full.at[f, rows], bs.at[w, k], br.at[w, k], seq, head)

        big_local.append(pltpu.make_async_copy(inp, full.at[h], wl.at[w]))
        mine = eighth(a, 0, 96)
        for k, other in enumerate((right, left)):
            big_x1.append(rcopy(inp.at[mine], full.at[h, mine], bs.at[w, k], br.at[w, k], me, other))
        big_x2.append(same(left, eighth(a, 0, 48), 2, me, right))
        big_x2.append(same(right, eighth(a, 48, 48), 3, me, left))
        for k, f in enumerate((left, right, opp)):
            big_a1[k].append(same(f, mine, 4 + k, along(1, 0), h))
            big_a1[k].append(same(f, mine, 7 + k, along(3, 0), h))
            big_a2[k].append(same(f, eighth(a_prev, 0, 48), 10 + k, along(1, 0), h))
            big_a2[k].append(same(f, eighth(a_next, 48, 48), 13 + k, along(3, 0), h))
            big_twin[k].append(same(f, half, 16 + k, sib, h))

    def start(copies):
        for copy in copies:
            copy.start()
            drains.append(copy.wait_send)

    def arrived(copies):
        for copy in copies:
            copy.wait_recv()

    all_first = fk_recv.at[pl.ds(1, NS - 1)]
    drains = [lambda: rcopy(all_first, all_first, fk_ss, fk_rs.at[0], me, right).wait_send()]
    for copy in [out_local] + big_local:
        copy.start()
    start(big_x1)

    for r in range(KD // 128):
        kc = jnp.broadcast_to(kept8[r:r + 1], (128, 128)).T
        sender = kc & (ND - 1)
        s_seq, s_head = lax.shift_right_arithmetic(sender, 2), sender & (NH - 1)
        within = lax.shift_right_arithmetic(kc, 7) - lax.shift_right_arithmetic(first - sender + (ND - 1), 7)
        way = (lax.shift_right_arithmetic(s_seq, 3) - ypos) & 3
        way = way * 4 + ((lax.shift_right_arithmetic(s_seq, 1) - zpos) & 3)
        words = [sum(CHIPS.index(divmod(8 * half + k, 4)) << (4 * k) for k in range(7)) for half in (0, 1)]
        last = [CHIPS.index(divmod(8 * half + 7, 4)) for half in (0, 1)]
        place = lax.shift_right_arithmetic(jnp.where(way < 8, words[0], words[1]), (way & 7) * 4) & 15
        place = jnp.where((way & 7) == 7, jnp.where(way < 8, last[0], last[1]), place)
        rel = place * 2 + ((s_seq + core) & 1)
        slot[r * 128:(r + 1) * 128] = (
            lax.shift_right_arithmetic(rel, 2) * (PER * NH) + s_head * PER + (rel & (PER - 1))
        ) * WIN + within

    feat_load.wait()

    def send_windows(g):
        lo = 1 if g == 0 else 0
        firsts = fk_recv.at[pl.ds(g * PER + lo, PER - lo)]
        rcopy(firsts, firsts, fk_ss, fk_rs.at[g], me, right).wait_recv()
        start = lax.shift_right_arithmetic(fk_recv[g * PER:(g + 1) * PER] - source + (ND - 1), 7)
        start = jnp.concatenate([start, start], axis=1).reshape(GROWS, 128)
        want = start + iota((GROWS, 128), 0) % WIN - iota((GROWS, 128), 1)
        pick = jnp.concatenate(
            [(want == t * 128).astype(F32).astype(BF) for t in range(ROWS // 128)], axis=1
        )
        send[g * GROWS:(g + 1) * GROWS] = dot(pick, feat[...]).astype(BF)
        for i in range(lo, PER):
            rcopy(
                send.at[pl.ds(g * GROWS + i * WIN, WIN)], recv.at[g, h, pl.ds(i * WIN, WIN)],
                s1_ss, s1_rs.at[g], offset(g * PER + i, -1), h,
            ).start()
        if g == 0:
            recv[0, h, 0:WIN] = send[0:WIN]

    sent = send.at[pl.ds(WIN, (NS - 1) * WIN)]
    drains.append(lambda: rcopy(sent, sent, s1_ss, s1_rs.at[0], me, right).wait_send())

    def arrive(g):
        lo = WIN if g == 0 else 0
        part = recv.at[g, h, pl.ds(lo, GROWS - lo)]
        rcopy(part, part, s1_ss, s1_rs.at[g], me, right).wait_recv()

    rings = []
    for g in range(GROUPS):
        rings.append((
            rcopy(recv.at[g, h], recv.at[g, h], xs.at[g, 0], xr.at[g, 0], me, right),
            rcopy(recv.at[g, h], recv.at[g, h], xs.at[g, 1], xr.at[g, 1], me, left),
            rcopy(recv.at[g, left, pl.ds(0, GROWS // 2)], recv.at[g, left, pl.ds(0, GROWS // 2)], xs.at[g, 2], xr.at[g, 2], me, right),
            rcopy(recv.at[g, right, pl.ds(GROWS // 2, GROWS // 2)], recv.at[g, right, pl.ds(GROWS // 2, GROWS // 2)], xs.at[g, 3], xr.at[g, 3], me, left),
        ))

    def compact(g):
        for k in (2 * g, 2 * g + 1):
            rings[k][2].wait_recv()
            rings[k][3].wait_recv()

        def block(b, c):
            at = pl.ds(pl.multiple_of(b * 512, 512), 512)
            want = slot[at] - g * 512 - iota((512, 128), 1)
            pick = jnp.concatenate([(want == t * 128).astype(F32).astype(BF) for t in range(4)], axis=1)
            got = dot(pick, recv[2 * g:2 * g + 2].reshape(512, D))
            if g == 0:
                dense[at] = got
            else:
                dense[at] = dense[at] + got
            return c

        lax.fori_loop(0, KD // 512, block, 0)

    def ring_pass(g):
        rings[g][0].wait_recv()
        rings[g][2].start()
        rings[g][1].wait_recv()
        rings[g][3].start()

    drains += [copy.wait_send for ring in rings for copy in ring]
    def ring_start(g):
        arrive(g)
        rings[g][0].start()
        rings[g][1].start()

    send_windows(0)
    send_windows(1)
    ring_start(0)
    send_windows(2)
    ring_start(1)
    send_windows(3)
    send_windows(4)
    ring_pass(0)
    ring_start(2)
    send_windows(5)
    send_windows(6)
    ring_pass(1)
    ring_start(3)
    send_windows(7)
    ring_pass(2)
    ring_start(4)
    arrived(big_x1)
    start(big_a1[0] + big_a1[1])
    qkv_load.wait()
    for j in range(HPD):
        low, high = j * 128, j * 128 + 64
        rows = slice(j * 64, j * 64 + 64)
        at_q, at_0 = (high, low) if v_first(j) else (low, high)
        wqkv[at_0:at_0 + 64] = jnp.zeros((64, D), BF)
        wqkv[at_q:at_q + 64] = (wraw[0, rows].astype(F32) * 0.125).astype(BF)
        wqkv[384 + at_q:384 + at_q + 64] = wraw[1, rows]
        wqkv[384 + at_0:384 + at_0 + 64] = wraw[2, rows]

    def turn(parts):
        for k in parts:
            at = slice(k * 128, (k + 1) * 128)
            wturn[:, at] = wqkv[at].astype(F32).T.astype(BF)

    turn((0, 1, 2))
    ring_pass(3)
    ring_start(5)
    turn((3, 4, 5))
    ring_pass(4)
    ring_start(6)
    ring_pass(5)
    ring_start(7)
    compact(0)
    arrived(big_a1[0] + big_a1[1])
    start(big_a2[0] + big_a2[1])
    ring_pass(6)
    compact(1)
    ring_pass(7)
    start(big_x2)
    start(out_mine)
    arrived(big_a2[0] + big_a2[1])
    start(big_twin[0] + big_twin[1])
    compact(2)
    compact(3)

    def norm(blk, c):
        block = layer_norm(dense[pl.ds(pl.multiple_of(blk * 256, 256), 256)], again).astype(BF)
        normed[pl.ds(pl.multiple_of(blk * 256, 256), 256)] = block
        row = iota((48, 256), 0)
        which = jnp.where(row < 16, foff[0], jnp.where(row < 32, foff[1], foff[2]))
        sel = (iota((48, 256), 1) == (row & 15) * 16 + which).astype(F32).astype(BF)
        rows = dot(sel, block).astype(BF)
        for j in range(HPD):
            nfar[j, pl.ds(pl.multiple_of(blk * 16, 16), 16)] = rows[j * 16:(j + 1) * 16]
        return c

    lax.fori_loop(0, KD // 256, norm, 0)
    for j in range(HPD):
        cols = slice(j * 128, (j + 1) * 128)
        farkv[core, ypos, zpos, :, cols] = dot(nfar[j], wturn[:, 384 + j * 128:512 + j * 128]).astype(BF)

    def far_copy(at, k, seq):
        return rcopy(farkv.at[at], farkv.at[at], fs.at[k], fr.at[k], seq, h)

    spots = (zpos, z_prev, z_next, (zpos + 2) % 4)
    far_a1 = [far_copy((core, ypos, zpos), 0, across(0, 1)), far_copy((core, ypos, zpos), 1, across(0, 3))]
    far_a2 = [
        far_copy((core, ypos, z_prev, pl.ds(0, 32)), 2, across(0, 1)),
        far_copy((core, ypos, z_next, pl.ds(32, 32)), 3, across(0, 3)),
    ]
    far_b1 = [
        [far_copy((core, ypos, x), 4 + 2 * k, across(1, 0)), far_copy((core, ypos, x), 5 + 2 * k, across(3, 0))]
        for k, x in enumerate(spots)
    ]
    far_b2 = [
        [
            far_copy((core, y_prev, x, pl.ds(0, 32)), 12 + 2 * k, across(1, 0)),
            far_copy((core, y_next, x, pl.ds(32, 32)), 13 + 2 * k, across(3, 0)),
        ]
        for k, x in enumerate(spots)
    ]
    far_twin = [far_copy((core, at), 20 + k, sib) for k, at in enumerate((ypos, y_prev, y_next, (ypos + 2) % 4))]
    mid_z = rcopy(midkv.at[core, zbit], midkv.at[core, zbit], ms.at[0], mr.at[0], zpart, h)
    mid_s = rcopy(midkv.at[core], midkv.at[core], ms.at[1], mr.at[1], sib, h)
    start(far_a1 + far_b1[0])

    def project_kv(blk, c):
        at = pl.ds(pl.multiple_of(blk * 512, 512), 512)
        kvb = dot(normed[at], wturn[:, 384:]).astype(BF)
        kv[at] = kvb
        at_m = pl.ds(pl.multiple_of(blk * 128, 128), 128)
        for j in range(HPD):
            cols = slice(j * 128, (j + 1) * 128)
            sel = (iota((128, 512), 1) == iota((128, 512), 0) * 4 + moff[j]).astype(F32).astype(BF)
            midkv[core, zbit, at_m, cols] = dot(sel, kvb[:, cols]).astype(BF)
        return c

    lax.fori_loop(0, KD // 512, project_kv, 0)
    start([mid_z])
    arrived(far_a1)
    start(far_a2 + far_b1[1] + far_b1[2])

    def project_q(blk, c):
        at = pl.ds(pl.multiple_of(blk * 512, 512), 512)
        qb = dot(normed[at], wturn[:, :384]).astype(BF)
        q[at] = qb
        at_m = pl.ds(pl.multiple_of(blk * 128, 128), 128)
        for j in range(HPD):
            cols = slice(j * 128, (j + 1) * 128)
            sel = (iota((128, 512), 1) == iota((128, 512), 0) * 4 + moff[j]).astype(F32).astype(BF)
            qmid[at_m, cols] = dot(sel, qb[:, cols]).astype(BF)
        return c

    lax.fori_loop(0, KD // 512, project_q, 0)
    for j in range(HPD):
        cols = slice(j * 128, (j + 1) * 128)
        qfar[:, cols] = dot(nfar[j], wturn[:, j * 128:(j + 1) * 128]).astype(BF)
    arrived(far_a2 + far_b1[0])
    start(far_b1[3] + far_b2[0] + far_twin[:1])

    def attend(qb, keys, j):
        scores = dot_nt(qb, keys)
        top = jnp.max(scores, axis=-1, keepdims=True)
        p = jnp.exp(scores - top)
        total = jnp.sum(p, axis=-1, keepdims=True)
        out = dot(p.astype(BF), keys)
        lane = iota(out.shape, 1)
        base = 64 if v_first(j) else 0
        out = jnp.where((lane >= base) & (lane < base + 32), top, out)
        return jnp.where((lane >= base + 32) & (lane < base + 64), total, out)

    def short(j, first_block):
        cols = slice(j * 128, (j + 1) * 128)

        at = slice(first_block * 256, first_block * 256 + 512)
        acc[j, at] = attend(q[at, cols], kv[:, cols], j)

    arrived(out_mine)
    start(out_ahead + out_twin[:2])
    short(0, 0)
    short(0, 2)
    arrived(far_b1[1] + far_b1[2])
    start(far_b2[1] + far_b2[2])
    short(1, 0)
    arrived(far_b1[3])
    start(far_b2[3] + far_twin[1:3])
    short(1, 2)
    arrived([mid_z])
    start([mid_s])
    arrived(out_ahead)
    start(out_twin[2:])
    short(2, 0)
    for k in range(4):
        arrived(far_b2[k])
    start(far_twin[3:])
    arrived(big_x2)
    start(big_a1[2])
    short(2, 2)
    arrived([mid_s])
    for j in range(HPD):
        cols = slice(j * 128, (j + 1) * 128)
        accm[j] = attend(qmid[:, cols], midkv[:, :, :, cols].reshape(KD, 128), j)
    arrived(far_twin)
    for j in range(HPD):
        cols = slice(j * 128, (j + 1) * 128)
        accf[j] = attend(qfar[:, cols], farkv[:, :, :, :, cols].reshape(2048, 128), j)

    arrived(big_a1[2])
    start(big_a2[2])
    def spread(one_hot, x):
        one = x.astype(BF)
        rest = x - one.astype(F32)
        two = rest.astype(BF)
        three = (rest - two.astype(F32)).astype(BF)
        return dot(one_hot, one) + dot(one_hot, two) + dot(one_hot, three)

    def merge(g):
        heads = []
        at = pl.ds(pl.multiple_of(g * 256, 256), 256)
        at_m = pl.ds(pl.multiple_of(g * 64, 64), 64)
        at_f = pl.ds(pl.multiple_of(g * 16, 16), 16)
        for j in range(HPD):
            base = 64 if v_first(j) else 0
            near = acc[j, at]
            hot_m = (iota((256, 64), 0) == iota((256, 64), 1) * 4 + moff[j]).astype(F32).astype(BF)
            hot_f = (iota((256, 16), 0) == iota((256, 16), 1) * 16 + foff[j]).astype(F32).astype(BF)
            middle = spread(hot_m, accm[j, at_m])
            far = spread(hot_f, accf[j, at_f])
            pos = iota((256, 1), 0)
            in_m = pos % 4 == moff[j]
            in_f = pos % 16 == foff[j]
            top_n = near[:, base:base + 1]
            top_m = jnp.where(in_m, middle[:, base:base + 1], NEG)
            top_f = jnp.where(in_f, far[:, base:base + 1], NEG)
            top = jnp.maximum(jnp.maximum(top_n, top_m), top_f)
            c_n = jnp.exp(top_n - top)
            c_m = jnp.exp(top_m - top)
            c_f = jnp.exp(top_f - top)
            under = (
                c_n * near[:, base + 32:base + 33]
                + c_m * middle[:, base + 32:base + 33]
                + c_f * far[:, base + 32:base + 33]
            )
            heads.append((c_n * near + c_m * middle + c_f * far) / under)
        lane = iota((256, 128), 1)
        lower = jnp.where(lane < 64, heads[0], heads[1])
        third = heads[2]
        upper = jnp.where(lane[:128] < 64, third[:128], pltpu.roll(third[128:], 64, 1))
        return lower.astype(BF), upper.astype(BF)

    swaps = []
    for r, g in enumerate((opp, right, left)):
        ho_send[r, :256], ho_send[r, 256:] = merge(g)
        swap = rcopy(ho_send.at[r], ho_recv.at[h], hs.at[r], hr.at[r], me, g)
        start([swap])
        swaps.append(swap)
    ho_recv[h, :256], ho_recv[h, 256:] = merge(h)
    arrived(big_a2[2])
    start(big_twin[2])
    out_local.wait()
    arrived(out_twin)
    arrived(swaps)
    attended = jnp.zeros((SHARE, D), F32)
    lane = iota((128, 128), 1)
    for g in range(NH):
        third = ho_recv[g, 256:]
        zero = jnp.zeros_like(third)
        third = jnp.concatenate([jnp.where(lane < 64, third, zero), jnp.where(lane < 64, zero, third)], axis=0)
        tail = outf[g, 128:]
        product = dot(ho_recv[g, :256], outf[g, :128]) + dot(third, jnp.concatenate([tail, tail], axis=0))
        attended = attended + product.astype(BF).astype(F32)
    residual = dense[pl.ds(pl.multiple_of(h * SHARE, SHARE), SHARE)] + attended
    normed_two = layer_norm(residual, mgain).astype(BF)
    for copy in big_local:
        copy.wait()
    arrived(big_twin[0] + big_twin[1] + big_twin[2])

    total = residual
    for g in range(NH):
        hidden = dot(normed_two, upf[g])
        hidden = (0.5 * hidden * (1.0 + lax.erf(hidden * 0.7071067811865476))).astype(BF)
        total = total + dot(hidden, downf[g]).astype(BF).astype(F32)
    o_ref[...] = total.astype(BF)

    for drain in drains:
        drain()


def local(tile_features, kept_tiles, attn_gain, qkv_weight, out_weight, middle_head_offset,
          far_head_offset, mlp_gain, up_weight, down_weight):
    vmem = pl.BlockSpec(memory_space=pltpu.VMEM)
    smem = pl.BlockSpec(memory_space=pltpu.SMEM)
    hbm = pl.BlockSpec(memory_space=pl.ANY)
    dma = pltpu.SemaphoreType.DMA
    return pl.pallas_call(
        kernel,
        out_shape=jax.ShapeDtypeStruct((SHARE, D), BF),
        in_specs=[smem, smem, vmem, vmem, vmem, hbm, hbm, hbm, hbm, hbm],
        out_specs=vmem,
        scratch_shapes=[
            pltpu.VMEM((ROWS, D), BF),
            pltpu.VMEM((3, 192, D), BF),
            pltpu.VMEM((D, D), BF),
            pltpu.VMEM((D, D), BF),
            pltpu.VMEM((NS * WIN, D), BF),
            pltpu.VMEM((GROUPS, NH, GROWS, D), BF),
            pltpu.VMEM((KD, 128), jnp.int32),
            pltpu.VMEM((KD, D), F32),
            pltpu.VMEM((KD, 384), BF),
            pltpu.VMEM((KD, 384), BF),
            pltpu.VMEM((256, 384), BF),
            pltpu.VMEM((64, 384), BF),
            pltpu.VMEM((KD, D), BF),
            pltpu.VMEM((HPD, 64, D), BF),
            pltpu.VMEM((2, 2, 256, 384), BF),
            pltpu.VMEM((2, 4, 4, 64, 384), BF),
            pltpu.VMEM((HPD, KD, 128), F32),
            pltpu.VMEM((HPD, 256, 128), F32),
            pltpu.VMEM((HPD, 64, 128), F32),
            pltpu.VMEM((3, 384, 128), BF),
            pltpu.VMEM((NH, 384, 128), BF),
            pltpu.VMEM((8, 128), jnp.int32),
            pltpu.VMEM((NS, 8, 128), jnp.int32),
            pltpu.VMEM((NH, D, D), BF),
            pltpu.VMEM((NH, D, D), BF),
            pltpu.VMEM((NH, 192, D), BF),
            dma, dma((GROUPS,)), dma, dma((GROUPS,)), dma((GROUPS, 4)), dma((GROUPS, 4)), dma((7,)), dma((7,)), dma((2, 19)), dma((2, 19)),
            dma((3,)), dma((2,)), dma((2,)), dma((2,)), dma((24,)), dma((24,)), dma((3,)), dma((3,)),
        ],
        compiler_params=pltpu.CompilerParams(
            collective_id=0, has_side_effects=True, vmem_limit_bytes=56 * 1024 * 1024
        ),
        cost_estimate=pl.CostEstimate(flops=12_000_000_000, bytes_accessed=20_000_000, transcendentals=5_000_000),
    )(
        middle_head_offset, far_head_offset, kept_tiles.reshape(8, 128), attn_gain.reshape(6, 128),
        mlp_gain.reshape(6, 128), tile_features, qkv_weight.transpose(1, 2, 0), up_weight, down_weight, out_weight,
    )


def solution(mesh):
    in_specs = (
        P(("seq", "head"), None),
        P("seq"),
        P(),
        P(None, None, "head"),
        P("head", None),
        P("head"),
        P("head"),
        P(),
        P(None, "head"),
        P("head", None),
    )
    out_specs = P(("seq", "head"), None)
    return jax.shard_map(local, mesh=mesh, in_specs=in_specs, out_specs=out_specs, check_vma=False)
```

```python
import functools

import jax
import jax.numpy as jnp
from jax import lax
from jax.experimental import pallas as pl
from jax.experimental.pallas import tpu as pltpu
from jax.sharding import PartitionSpec as P

NS = 32
NH = 4
ND = NS * NH
D = 768
KD = 1024
HD = 64
HPD = 3
WIN = 16
GROUPS = 8
PER = NS // GROUPS
GROWS = PER * WIN
ROWS = 640
SHARE = KD // NH
EPS = 1e-05
NEG = -1e30
CHIPS = (
    (0, 0), (0, 1), (0, 3), (1, 0), (3, 0), (1, 1), (1, 3), (3, 1),
    (3, 3), (0, 2), (2, 0), (1, 2), (2, 1), (2, 3), (3, 2), (2, 2),
)
PLACES = tuple((dy, dz, dc) for dy, dz in CHIPS for dc in (0, 1))
BF = jnp.bfloat16
F32 = jnp.float32


def dot(a, b):
    return lax.dot_general(a, b, (((1,), (0,)), ((), ())), preferred_element_type=F32)


def dot_nt(a, b):
    return lax.dot_general(a, b, (((1,), (1,)), ((), ())), preferred_element_type=F32)


def layer_norm(x, gain):
    centred = x - jnp.mean(x, axis=-1, keepdims=True)
    variance = jnp.mean(centred * centred, axis=-1, keepdims=True)
    return centred * lax.rsqrt(variance + EPS) * gain


def iota(shape, axis):
    return lax.broadcasted_iota(jnp.int32, shape, axis)


def v_first(head):
    return head != 1


def kernel(
    moff, foff, kept8, again6, mgain6, feat_in, qkv_in, up, down, outw,
    o_ref,
    feat, wraw, wqkv, wturn, send, recv, slot, dense, q, kv, qmid, qfar, normed, nfar, midkv, farkv, acc, accm, accf,
    ho_send, ho_recv, fk_send, fk_recv, upf, downf, outf,
    fk_ss, fk_rs, s1_ss, s1_rs, xs, xr, os, orr, bs, br, wl, ls, ms, mr, fs, fr, hs, hr,
):
    me = lax.axis_index("seq")
    h = lax.axis_index("head")
    right, left, opp = (h + 1) % NH, (h + 3) % NH, (h + 2) % NH
    core = me % 2
    chip = me // 2
    sib = me + 1 - 2 * core
    zbit = chip % 2
    zpart = me + 2 - 4 * zbit
    source = me * NH + h
    ypos, zpos = chip // 4, chip % 4
    a = ypos * (1 - core) + zpos * core
    b = zpos * (1 - core) + ypos * core
    a_next, a_prev, b_next, b_prev, b_opp = (a + 1) % 4, (a + 3) % 4, (b + 1) % 4, (b + 3) % 4, (b + 2) % 4

    def along(da, db):
        y = (ypos + (1 - core) * da + core * db) % 4
        z = (zpos + core * da + (1 - core) * db) % 4
        return (y * 4 + z) * 2 + core


    y_next, y_prev, z_next, z_prev = (ypos + 1) % 4, (ypos + 3) % 4, (zpos + 1) % 4, (zpos + 3) % 4

    def across(dy, dz):
        return ((ypos + dy) % 4 * 4 + (zpos + dz) % 4) * 2 + core

    def offset(n, sign):
        dy, dz, dc = PLACES[n]
        return ((ypos + sign * dy) % 4 * 4 + (zpos + sign * dz) % 4) * 2 + (core + dc) % 2

    def rcopy(src, dst, ssem, rsem, seq, head):
        return pltpu.make_async_remote_copy(
            src_ref=src, dst_ref=dst, send_sem=ssem, recv_sem=rsem,
            device_id=(seq, head), device_id_type=pl.DeviceIdType.MESH,
        )

    feat_load = pltpu.make_async_copy(feat_in, feat, ls.at[0])
    feat_load.start()
    qkv_load = pltpu.make_async_copy(qkv_in, wraw, ls.at[1])
    qkv_load.start()
    again = jnp.concatenate([again6[k:k + 1] for k in range(6)], axis=1)
    mgain = jnp.concatenate([mgain6[k:k + 1] for k in range(6)], axis=1)

    barrier = pltpu.get_barrier_semaphore()

    for n in range(1, NS):
        pl.semaphore_signal(barrier, inc=1, device_id=(offset(n, 1), h), device_id_type=pl.DeviceIdType.MESH)
    for other in (right, left, opp):
        pl.semaphore_signal(barrier, inc=1, device_id=(me, other), device_id_type=pl.DeviceIdType.MESH)
    first = kept8[0:1, 0:1]
    fk_send[...] = jnp.broadcast_to(first, (8, 128))
    fk_recv[0] = fk_send[...]
    pl.semaphore_wait(barrier, NS - 1 + NH - 1)

    for n in range(1, NS):
        rcopy(fk_send, fk_recv.at[n], fk_ss, fk_rs.at[n // PER], offset(n, 1), h).start()

    out_local = pltpu.make_async_copy(outw, outf.at[h], wl.at[2])
    lo = pl.multiple_of(core * 96, 16)
    own = pl.ds(lo, 96)
    out_mine = [
        rcopy(outw.at[own], outf.at[h, own], os.at[0], orr.at[0], me, right),
        rcopy(outw.at[own], outf.at[h, own], os.at[1], orr.at[1], me, left),
    ]
    at_l, at_r = pl.ds(lo, 48), pl.ds(pl.multiple_of(core * 96 + 48, 16), 48)
    out_ahead = [
        rcopy(outf.at[left, at_l], outf.at[left, at_l], os.at[2], orr.at[2], me, right),
        rcopy(outf.at[right, at_r], outf.at[right, at_r], os.at[3], orr.at[3], me, left),
    ]
    out_twin = [
        rcopy(outf.at[f, own], outf.at[f, own], os.at[4 + k], orr.at[4 + k], sib, h)
        for k, f in enumerate((left, right, opp))
    ]

    def eighth(at, skip, count):
        return pl.ds(pl.multiple_of(core * 384 + at * 96 + skip, 16), count)

    half = pl.ds(pl.multiple_of(core * 384, 16), 384)
    big_local, big_x1, big_x2, big_a1, big_a2, big_twin = [], [], [], [[], [], []], [[], [], []], [[], [], []]
    for w, (inp, full) in enumerate(((up, upf), (down, downf))):
        def same(f, rows, k, seq, head):
            return rcopy(full.at[f, rows], full.at[f, rows], bs.at[w, k], br.at[w, k], seq, head)

        big_local.append(pltpu.make_async_copy(inp, full.at[h], wl.at[w]))
        mine = eighth(a, 0, 96)
        for k, other in enumerate((right, left)):
            big_x1.append(rcopy(inp.at[mine], full.at[h, mine], bs.at[w, k], br.at[w, k], me, other))
        big_x2.append(same(left, eighth(a, 0, 48), 2, me, right))
        big_x2.append(same(right, eighth(a, 48, 48), 3, me, left))
        for k, f in enumerate((left, right, opp)):
            big_a1[k].append(same(f, mine, 4 + k, along(1, 0), h))
            big_a1[k].append(same(f, mine, 7 + k, along(3, 0), h))
            big_a2[k].append(same(f, eighth(a_prev, 0, 48), 10 + k, along(1, 0), h))
            big_a2[k].append(same(f, eighth(a_next, 48, 48), 13 + k, along(3, 0), h))
            big_twin[k].append(same(f, half, 16 + k, sib, h))

    def start(copies):
        for copy in copies:
            copy.start()
            drains.append(copy.wait_send)

    def arrived(copies):
        for copy in copies:
            copy.wait_recv()

    all_first = fk_recv.at[pl.ds(1, NS - 1)]
    drains = [lambda: rcopy(all_first, all_first, fk_ss, fk_rs.at[0], me, right).wait_send()]
    for copy in [out_local] + big_local:
        copy.start()
    start(big_x1)

    for r in range(KD // 128):
        kc = jnp.broadcast_to(kept8[r:r + 1], (128, 128)).T
        sender = kc & (ND - 1)
        s_seq, s_head = lax.shift_right_arithmetic(sender, 2), sender & (NH - 1)
        within = lax.shift_right_arithmetic(kc, 7) - lax.shift_right_arithmetic(first - sender + (ND - 1), 7)
        way = (lax.shift_right_arithmetic(s_seq, 3) - ypos) & 3
        way = way * 4 + ((lax.shift_right_arithmetic(s_seq, 1) - zpos) & 3)
        words = [sum(CHIPS.index(divmod(8 * half + k, 4)) << (4 * k) for k in range(7)) for half in (0, 1)]
        last = [CHIPS.index(divmod(8 * half + 7, 4)) for half in (0, 1)]
        place = lax.shift_right_arithmetic(jnp.where(way < 8, words[0], words[1]), (way & 7) * 4) & 15
        place = jnp.where((way & 7) == 7, jnp.where(way < 8, last[0], last[1]), place)
        rel = place * 2 + ((s_seq + core) & 1)
        slot[r * 128:(r + 1) * 128] = (
            lax.shift_right_arithmetic(rel, 2) * (PER * NH) + s_head * PER + (rel & (PER - 1))
        ) * WIN + within

    feat_load.wait()

    def send_windows(g):
        lo = 1 if g == 0 else 0
        firsts = fk_recv.at[pl.ds(g * PER + lo, PER - lo)]
        rcopy(firsts, firsts, fk_ss, fk_rs.at[g], me, right).wait_recv()
        start = lax.shift_right_arithmetic(fk_recv[g * PER:(g + 1) * PER] - source + (ND - 1), 7)
        start = jnp.concatenate([start, start], axis=1).reshape(GROWS, 128)
        want = start + iota((GROWS, 128), 0) % WIN - iota((GROWS, 128), 1)
        pick = jnp.concatenate(
            [(want == t * 128).astype(F32).astype(BF) for t in range(ROWS // 128)], axis=1
        )
        send[g * GROWS:(g + 1) * GROWS] = dot(pick, feat[...]).astype(BF)
        for i in range(lo, PER):
            rcopy(
                send.at[pl.ds(g * GROWS + i * WIN, WIN)], recv.at[g, h, pl.ds(i * WIN, WIN)],
                s1_ss, s1_rs.at[g], offset(g * PER + i, -1), h,
            ).start()
        if g == 0:
            recv[0, h, 0:WIN] = send[0:WIN]

    sent = send.at[pl.ds(WIN, (NS - 1) * WIN)]
    drains.append(lambda: rcopy(sent, sent, s1_ss, s1_rs.at[0], me, right).wait_send())

    def arrive(g):
        lo = WIN if g == 0 else 0
        part = recv.at[g, h, pl.ds(lo, GROWS - lo)]
        rcopy(part, part, s1_ss, s1_rs.at[g], me, right).wait_recv()

    rings = []
    for g in range(GROUPS):
        rings.append((
            rcopy(recv.at[g, h], recv.at[g, h], xs.at[g, 0], xr.at[g, 0], me, right),
            rcopy(recv.at[g, h], recv.at[g, h], xs.at[g, 1], xr.at[g, 1], me, left),
            rcopy(recv.at[g, left, pl.ds(0, GROWS // 2)], recv.at[g, left, pl.ds(0, GROWS // 2)], xs.at[g, 2], xr.at[g, 2], me, right),
            rcopy(recv.at[g, right, pl.ds(GROWS // 2, GROWS // 2)], recv.at[g, right, pl.ds(GROWS // 2, GROWS // 2)], xs.at[g, 3], xr.at[g, 3], me, left),
        ))

    def compact(g):
        for k in (2 * g, 2 * g + 1):
            rings[k][2].wait_recv()
            rings[k][3].wait_recv()

        def block(b, c):
            at = pl.ds(pl.multiple_of(b * 512, 512), 512)
            want = slot[at] - g * 512 - iota((512, 128), 1)
            pick = jnp.concatenate([(want == t * 128).astype(F32).astype(BF) for t in range(4)], axis=1)
            got = dot(pick, recv[2 * g:2 * g + 2].reshape(512, D))
            if g == 0:
                dense[at] = got
            else:
                dense[at] = dense[at] + got
            return c

        lax.fori_loop(0, KD // 512, block, 0)

    def ring_pass(g):
        rings[g][0].wait_recv()
        rings[g][2].start()
        rings[g][1].wait_recv()
        rings[g][3].start()

    drains += [copy.wait_send for ring in rings for copy in ring]
    def ring_start(g):
        arrive(g)
        rings[g][0].start()
        rings[g][1].start()

    send_windows(0)
    send_windows(1)
    ring_start(0)
    send_windows(2)
    ring_start(1)
    send_windows(3)
    send_windows(4)
    ring_pass(0)
    ring_start(2)
    send_windows(5)
    send_windows(6)
    ring_pass(1)
    ring_start(3)
    send_windows(7)
    ring_pass(2)
    ring_start(4)
    arrived(big_x1)
    start(big_a1[0] + big_a1[1])
    qkv_load.wait()
    for j in range(HPD):
        low, high = j * 128, j * 128 + 64
        rows = slice(j * 64, j * 64 + 64)
        at_q, at_0 = (high, low) if v_first(j) else (low, high)
        wqkv[at_0:at_0 + 64] = jnp.zeros((64, D), BF)
        wqkv[at_q:at_q + 64] = (wraw[0, rows].astype(F32) * 0.125).astype(BF)
        wqkv[384 + at_q:384 + at_q + 64] = wraw[1, rows]
        wqkv[384 + at_0:384 + at_0 + 64] = wraw[2, rows]

    def turn(parts):
        for k in parts:
            at = slice(k * 128, (k + 1) * 128)
            wturn[:, at] = wqkv[at].astype(F32).T.astype(BF)

    turn((0, 1, 2))
    ring_pass(3)
    ring_start(5)
    turn((3, 4, 5))
    ring_pass(4)
    ring_start(6)
    ring_pass(5)
    ring_start(7)
    compact(0)
    arrived(big_a1[0] + big_a1[1])
    start(big_a2[0] + big_a2[1])
    ring_pass(6)
    compact(1)
    ring_pass(7)
    start(big_x2)
    start(out_mine)
    arrived(big_a2[0] + big_a2[1])
    start(big_twin[0] + big_twin[1])
    compact(2)
    compact(3)

    def norm(blk, c):
        block = layer_norm(dense[pl.ds(pl.multiple_of(blk * 256, 256), 256)], again).astype(BF)
        normed[pl.ds(pl.multiple_of(blk * 256, 256), 256)] = block
        row = iota((48, 256), 0)
        which = jnp.where(row < 16, foff[0], jnp.where(row < 32, foff[1], foff[2]))
        sel = (iota((48, 256), 1) == (row & 15) * 16 + which).astype(F32).astype(BF)
        rows = dot(sel, block).astype(BF)
        for j in range(HPD):
            nfar[j, pl.ds(pl.multiple_of(blk * 16, 16), 16)] = rows[j * 16:(j + 1) * 16]
        return c

    lax.fori_loop(0, KD // 256, norm, 0)
    for j in range(HPD):
        cols = slice(j * 128, (j + 1) * 128)
        farkv[core, ypos, zpos, :, cols] = dot(nfar[j], wturn[:, 384 + j * 128:512 + j * 128]).astype(BF)

    def far_copy(at, k, seq):
        return rcopy(farkv.at[at], farkv.at[at], fs.at[k], fr.at[k], seq, h)

    spots = (zpos, z_prev, z_next, (zpos + 2) % 4)
    far_a1 = [far_copy((core, ypos, zpos), 0, across(0, 1)), far_copy((core, ypos, zpos), 1, across(0, 3))]
    far_a2 = [
        far_copy((core, ypos, z_prev, pl.ds(0, 32)), 2, across(0, 1)),
        far_copy((core, ypos, z_next, pl.ds(32, 32)), 3, across(0, 3)),
    ]
    far_b1 = [
        [far_copy((core, ypos, x), 4 + 2 * k, across(1, 0)), far_copy((core, ypos, x), 5 + 2 * k, across(3, 0))]
        for k, x in enumerate(spots)
    ]
    far_b2 = [
        [
            far_copy((core, y_prev, x, pl.ds(0, 32)), 12 + 2 * k, across(1, 0)),
            far_copy((core, y_next, x, pl.ds(32, 32)), 13 + 2 * k, across(3, 0)),
        ]
        for k, x in enumerate(spots)
    ]
    far_twin = [far_copy((core, at), 20 + k, sib) for k, at in enumerate((ypos, y_prev, y_next, (ypos + 2) % 4))]
    mid_z = rcopy(midkv.at[core, zbit], midkv.at[core, zbit], ms.at[0], mr.at[0], zpart, h)
    mid_s = rcopy(midkv.at[core], midkv.at[core], ms.at[1], mr.at[1], sib, h)
    start(far_a1 + far_b1[0])

    def project_kv(blk, c):
        at = pl.ds(pl.multiple_of(blk * 512, 512), 512)
        kvb = dot(normed[at], wturn[:, 384:]).astype(BF)
        kv[at] = kvb
        at_m = pl.ds(pl.multiple_of(blk * 128, 128), 128)
        for j in range(HPD):
            cols = slice(j * 128, (j + 1) * 128)
            sel = (iota((128, 512), 1) == iota((128, 512), 0) * 4 + moff[j]).astype(F32).astype(BF)
            midkv[core, zbit, at_m, cols] = dot(sel, kvb[:, cols]).astype(BF)
        return c

    lax.fori_loop(0, KD // 512, project_kv, 0)
    start([mid_z])
    arrived(far_a1)
    start(far_a2 + far_b1[1] + far_b1[2])

    def project_q(blk, c):
        at = pl.ds(pl.multiple_of(blk * 512, 512), 512)
        qb = dot(normed[at], wturn[:, :384]).astype(BF)
        q[at] = qb
        at_m = pl.ds(pl.multiple_of(blk * 128, 128), 128)
        for j in range(HPD):
            cols = slice(j * 128, (j + 1) * 128)
            sel = (iota((128, 512), 1) == iota((128, 512), 0) * 4 + moff[j]).astype(F32).astype(BF)
            qmid[at_m, cols] = dot(sel, qb[:, cols]).astype(BF)
        return c

    lax.fori_loop(0, KD // 512, project_q, 0)
    for j in range(HPD):
        cols = slice(j * 128, (j + 1) * 128)
        qfar[:, cols] = dot(nfar[j], wturn[:, j * 128:(j + 1) * 128]).astype(BF)
    arrived(far_a2 + far_b1[0])
    start(far_b1[3] + far_b2[0] + far_twin[:1])

    def attend(qb, keys, j):
        scores = dot_nt(qb, keys)
        top = jnp.max(scores, axis=-1, keepdims=True)
        p = jnp.exp(scores - top)
        total = jnp.sum(p, axis=-1, keepdims=True)
        out = dot(p.astype(BF), keys)
        lane = iota(out.shape, 1)
        base = 64 if v_first(j) else 0
        out = jnp.where((lane >= base) & (lane < base + 32), top, out)
        return jnp.where((lane >= base + 32) & (lane < base + 64), total, out)

    def short(j, first_block):
        cols = slice(j * 128, (j + 1) * 128)

        at = slice(first_block * 256, first_block * 256 + 512)
        acc[j, at] = attend(q[at, cols], kv[:, cols], j)

    arrived(out_mine)
    start(out_ahead + out_twin[:2])
    short(0, 0)
    short(0, 2)
    arrived(far_b1[1] + far_b1[2])
    start(far_b2[1] + far_b2[2])
    short(1, 0)
    arrived(far_b1[3])
    start(far_b2[3] + far_twin[1:3])
    short(1, 2)
    arrived([mid_z])
    start([mid_s])
    arrived(out_ahead)
    start(out_twin[2:])
    short(2, 0)
    for k in range(4):
        arrived(far_b2[k])
    start(far_twin[3:])
    arrived(big_x2)
    start(big_a1[2])
    short(2, 2)
    arrived([mid_s])
    for j in range(HPD):
        cols = slice(j * 128, (j + 1) * 128)
        accm[j] = attend(qmid[:, cols], midkv[:, :, :, cols].reshape(KD, 128), j)
    arrived(far_twin)
    for j in range(HPD):
        cols = slice(j * 128, (j + 1) * 128)
        accf[j] = attend(qfar[:, cols], farkv[:, :, :, :, cols].reshape(2048, 128), j)

    def spread(one_hot, x):
        one = x.astype(BF)
        rest = x - one.astype(F32)
        two = rest.astype(BF)
        three = (rest - two.astype(F32)).astype(BF)
        return dot(one_hot, one) + dot(one_hot, two) + dot(one_hot, three)

    def merge(g):
        heads = []
        at = pl.ds(pl.multiple_of(g * 256, 256), 256)
        at_m = pl.ds(pl.multiple_of(g * 64, 64), 64)
        at_f = pl.ds(pl.multiple_of(g * 16, 16), 16)
        for j in range(HPD):
            base = 64 if v_first(j) else 0
            near = acc[j, at]
            hot_m = (iota((256, 64), 0) == iota((256, 64), 1) * 4 + moff[j]).astype(F32).astype(BF)
            hot_f = (iota((256, 16), 0) == iota((256, 16), 1) * 16 + foff[j]).astype(F32).astype(BF)
            middle = spread(hot_m, accm[j, at_m])
            far = spread(hot_f, accf[j, at_f])
            pos = iota((256, 1), 0)
            in_m = pos % 4 == moff[j]
            in_f = pos % 16 == foff[j]
            top_n = near[:, base:base + 1]
            top_m = jnp.where(in_m, middle[:, base:base + 1], NEG)
            top_f = jnp.where(in_f, far[:, base:base + 1], NEG)
            top = jnp.maximum(jnp.maximum(top_n, top_m), top_f)
            c_n = jnp.exp(top_n - top)
            c_m = jnp.exp(top_m - top)
            c_f = jnp.exp(top_f - top)
            under = (
                c_n * near[:, base + 32:base + 33]
                + c_m * middle[:, base + 32:base + 33]
                + c_f * far[:, base + 32:base + 33]
            )
            heads.append((c_n * near + c_m * middle + c_f * far) / under)
        lane = iota((256, 128), 1)
        lower = jnp.where(lane < 64, heads[0], heads[1])
        third = heads[2]
        upper = jnp.where(lane[:128] < 64, third[:128], pltpu.roll(third[128:], 64, 1))
        return lower.astype(BF), upper.astype(BF)

    swaps = []
    for r, g in enumerate((opp, right, left)):
        ho_send[r, :256], ho_send[r, 256:] = merge(g)
        swap = rcopy(ho_send.at[r], ho_recv.at[h], hs.at[r], hr.at[r], me, g)
        start([swap])
        swaps.append(swap)
        if r == 1:
            arrived(big_a1[2])
            start(big_a2[2])
    ho_recv[h, :256], ho_recv[h, 256:] = merge(h)
    arrived(big_a2[2])
    start(big_twin[2])
    out_local.wait()
    arrived(out_twin)
    attended = jnp.zeros((SHARE, D), F32)
    lane = iota((128, 128), 1)
    for g, swap in ((h, []), (left, swaps[1:2]), (right, swaps[2:]), (opp, swaps[:1])):
        arrived(swap)
        third = ho_recv[g, 256:]
        zero = jnp.zeros_like(third)
        third = jnp.concatenate([jnp.where(lane < 64, third, zero), jnp.where(lane < 64, zero, third)], axis=0)
        tail = outf[g, 128:]
        product = dot(ho_recv[g, :256], outf[g, :128]) + dot(third, jnp.concatenate([tail, tail], axis=0))
        attended = attended + product.astype(BF).astype(F32)
    residual = dense[pl.ds(pl.multiple_of(h * SHARE, SHARE), SHARE)] + attended
    normed_two = layer_norm(residual, mgain).astype(BF)
    for copy in big_local:
        copy.wait()

    total = residual
    for g, twin in ((h, []), (left, big_twin[0]), (right, big_twin[1]), (opp, big_twin[2])):
        arrived(twin)
        hidden = dot(normed_two, upf[g])
        hidden = (0.5 * hidden * (1.0 + lax.erf(hidden * 0.7071067811865476))).astype(BF)
        total = total + dot(hidden, downf[g]).astype(BF).astype(F32)
    o_ref[...] = total.astype(BF)

    for drain in drains:
        drain()


def local(tile_features, kept_tiles, attn_gain, qkv_weight, out_weight, middle_head_offset,
          far_head_offset, mlp_gain, up_weight, down_weight):
    vmem = pl.BlockSpec(memory_space=pltpu.VMEM)
    smem = pl.BlockSpec(memory_space=pltpu.SMEM)
    hbm = pl.BlockSpec(memory_space=pl.ANY)
    dma = pltpu.SemaphoreType.DMA
    return pl.pallas_call(
        kernel,
        out_shape=jax.ShapeDtypeStruct((SHARE, D), BF),
        in_specs=[smem, smem, vmem, vmem, vmem, hbm, hbm, hbm, hbm, hbm],
        out_specs=vmem,
        scratch_shapes=[
            pltpu.VMEM((ROWS, D), BF),
            pltpu.VMEM((3, 192, D), BF),
            pltpu.VMEM((D, D), BF),
            pltpu.VMEM((D, D), BF),
            pltpu.VMEM((NS * WIN, D), BF),
            pltpu.VMEM((GROUPS, NH, GROWS, D), BF),
            pltpu.VMEM((KD, 128), jnp.int32),
            pltpu.VMEM((KD, D), F32),
            pltpu.VMEM((KD, 384), BF),
            pltpu.VMEM((KD, 384), BF),
            pltpu.VMEM((256, 384), BF),
            pltpu.VMEM((64, 384), BF),
            pltpu.VMEM((KD, D), BF),
            pltpu.VMEM((HPD, 64, D), BF),
            pltpu.VMEM((2, 2, 256, 384), BF),
            pltpu.VMEM((2, 4, 4, 64, 384), BF),
            pltpu.VMEM((HPD, KD, 128), F32),
            pltpu.VMEM((HPD, 256, 128), F32),
            pltpu.VMEM((HPD, 64, 128), F32),
            pltpu.VMEM((3, 384, 128), BF),
            pltpu.VMEM((NH, 384, 128), BF),
            pltpu.VMEM((8, 128), jnp.int32),
            pltpu.VMEM((NS, 8, 128), jnp.int32),
            pltpu.VMEM((NH, D, D), BF),
            pltpu.VMEM((NH, D, D), BF),
            pltpu.VMEM((NH, 192, D), BF),
            dma, dma((GROUPS,)), dma, dma((GROUPS,)), dma((GROUPS, 4)), dma((GROUPS, 4)), dma((7,)), dma((7,)), dma((2, 19)), dma((2, 19)),
            dma((3,)), dma((2,)), dma((2,)), dma((2,)), dma((24,)), dma((24,)), dma((3,)), dma((3,)),
        ],
        compiler_params=pltpu.CompilerParams(
            collective_id=0, has_side_effects=True, vmem_limit_bytes=56 * 1024 * 1024
        ),
        cost_estimate=pl.CostEstimate(flops=12_000_000_000, bytes_accessed=20_000_000, transcendentals=5_000_000),
    )(
        middle_head_offset, far_head_offset, kept_tiles.reshape(8, 128), attn_gain.reshape(6, 128),
        mlp_gain.reshape(6, 128), tile_features, qkv_weight.transpose(1, 2, 0), up_weight, down_weight, out_weight,
    )


def solution(mesh):
    in_specs = (
        P(("seq", "head"), None),
        P("seq"),
        P(),
        P(None, None, "head"),
        P("head", None),
        P("head"),
        P("head"),
        P(),
        P(None, "head"),
        P("head", None),
    )
    out_specs = P(("seq", "head"), None)
    return jax.shard_map(local, mesh=mesh, in_specs=in_specs, out_specs=out_specs, check_vma=False)
```

```python
import functools

import jax
import jax.numpy as jnp
from jax import lax
from jax.experimental import pallas as pl
from jax.experimental.pallas import tpu as pltpu
from jax.sharding import PartitionSpec as P

NS = 32
NH = 4
ND = NS * NH
D = 768
KD = 1024
HD = 64
HPD = 3
WIN = 16
GROUPS = 8
PER = NS // GROUPS
GROWS = PER * WIN
ROWS = 640
SHARE = KD // NH
EPS = 1e-05
NEG = -1e30
CHIPS = (
    (0, 0), (0, 1), (0, 3), (1, 0), (3, 0), (1, 1), (1, 3), (3, 1),
    (3, 3), (0, 2), (2, 0), (1, 2), (2, 1), (2, 3), (3, 2), (2, 2),
)
PLACES = tuple((dy, dz, dc) for dy, dz in CHIPS for dc in (0, 1))
BF = jnp.bfloat16
F32 = jnp.float32


def dot(a, b):
    return lax.dot_general(a, b, (((1,), (0,)), ((), ())), preferred_element_type=F32)


def dot_nt(a, b):
    return lax.dot_general(a, b, (((1,), (1,)), ((), ())), preferred_element_type=F32)


def layer_norm(x, gain):
    centred = x - jnp.mean(x, axis=-1, keepdims=True)
    variance = jnp.mean(centred * centred, axis=-1, keepdims=True)
    return centred * lax.rsqrt(variance + EPS) * gain


def iota(shape, axis):
    return lax.broadcasted_iota(jnp.int32, shape, axis)


def v_first(head):
    return head != 1


def kernel(
    moff, foff, kept8, again6, mgain6, feat_in, qkv_in, up, down, outw,
    o_ref,
    feat, wraw, wqkv, wturn, send, recv, slot, dense, q, kv, qmid, qfar, normed, nfar, midkv, farkv, acc, accm, accf,
    ho_send, ho_recv, fk_send, fk_recv, upf, downf, outf,
    fk_ss, fk_rs, s1_ss, s1_rs, xs, xr, os, orr, bs, br, wl, ls, ms, mr, fs, fr, hs, hr,
):
    me = lax.axis_index("seq")
    h = lax.axis_index("head")
    right, left, opp = (h + 1) % NH, (h + 3) % NH, (h + 2) % NH
    core = me % 2
    chip = me // 2
    sib = me + 1 - 2 * core
    zbit = chip % 2
    zpart = me + 2 - 4 * zbit
    source = me * NH + h
    ypos, zpos = chip // 4, chip % 4
    a = ypos * (1 - core) + zpos * core
    b = zpos * (1 - core) + ypos * core
    a_next, a_prev, b_next, b_prev, b_opp = (a + 1) % 4, (a + 3) % 4, (b + 1) % 4, (b + 3) % 4, (b + 2) % 4

    def along(da, db):
        y = (ypos + (1 - core) * da + core * db) % 4
        z = (zpos + core * da + (1 - core) * db) % 4
        return (y * 4 + z) * 2 + core


    y_next, y_prev, z_next, z_prev = (ypos + 1) % 4, (ypos + 3) % 4, (zpos + 1) % 4, (zpos + 3) % 4

    def across(dy, dz):
        return ((ypos + dy) % 4 * 4 + (zpos + dz) % 4) * 2 + core

    def offset(n, sign):
        dy, dz, dc = PLACES[n]
        return ((ypos + sign * dy) % 4 * 4 + (zpos + sign * dz) % 4) * 2 + (core + dc) % 2

    def rcopy(src, dst, ssem, rsem, seq, head):
        return pltpu.make_async_remote_copy(
            src_ref=src, dst_ref=dst, send_sem=ssem, recv_sem=rsem,
            device_id=(seq, head), device_id_type=pl.DeviceIdType.MESH,
        )

    feat_load = pltpu.make_async_copy(feat_in, feat, ls.at[0])
    feat_load.start()
    qkv_load = pltpu.make_async_copy(qkv_in, wraw, ls.at[1])
    qkv_load.start()
    again = jnp.concatenate([again6[k:k + 1] for k in range(6)], axis=1)
    mgain = jnp.concatenate([mgain6[k:k + 1] for k in range(6)], axis=1)

    barrier = pltpu.get_barrier_semaphore()

    for n in range(1, NS):
        pl.semaphore_signal(barrier, inc=1, device_id=(offset(n, 1), h), device_id_type=pl.DeviceIdType.MESH)
    for other in (right, left, opp):
        pl.semaphore_signal(barrier, inc=1, device_id=(me, other), device_id_type=pl.DeviceIdType.MESH)
    first = kept8[0:1, 0:1]
    fk_send[...] = jnp.broadcast_to(first, (8, 128))
    fk_recv[0] = fk_send[...]
    pl.semaphore_wait(barrier, NS - 1 + NH - 1)

    for n in range(1, NS):
        rcopy(fk_send, fk_recv.at[n], fk_ss, fk_rs.at[n // PER], offset(n, 1), h).start()

    out_local = pltpu.make_async_copy(outw, outf.at[h], wl.at[2])
    lo = pl.multiple_of(core * 96, 16)
    own = pl.ds(lo, 96)
    out_mine = [
        rcopy(outw.at[own], outf.at[h, own], os.at[0], orr.at[0], me, right),
        rcopy(outw.at[own], outf.at[h, own], os.at[1], orr.at[1], me, left),
    ]
    at_l, at_r = pl.ds(lo, 48), pl.ds(pl.multiple_of(core * 96 + 48, 16), 48)
    out_ahead = [
        rcopy(outf.at[left, at_l], outf.at[left, at_l], os.at[2], orr.at[2], me, right),
        rcopy(outf.at[right, at_r], outf.at[right, at_r], os.at[3], orr.at[3], me, left),
    ]
    out_twin = [
        rcopy(outf.at[f, own], outf.at[f, own], os.at[4 + k], orr.at[4 + k], sib, h)
        for k, f in enumerate((left, right, opp))
    ]

    def eighth(at, skip, count):
        return pl.ds(pl.multiple_of(core * 384 + at * 96 + skip, 16), count)

    half = pl.ds(pl.multiple_of(core * 384, 16), 384)
    big_local, big_x1, big_x2, big_a1, big_a2, big_twin = [], [], [], [[], [], []], [[], [], []], [[], [], []]
    for w, (inp, full) in enumerate(((up, upf), (down, downf))):
        def same(f, rows, k, seq, head):
            return rcopy(full.at[f, rows], full.at[f, rows], bs.at[w, k], br.at[w, k], seq, head)

        big_local.append(pltpu.make_async_copy(inp, full.at[h], wl.at[w]))
        mine = eighth(a, 0, 96)
        for k, other in enumerate((right, left)):
            big_x1.append(rcopy(inp.at[mine], full.at[h, mine], bs.at[w, k], br.at[w, k], me, other))
        big_x2.append(same(left, eighth(a, 0, 48), 2, me, right))
        big_x2.append(same(right, eighth(a, 48, 48), 3, me, left))
        for k, f in enumerate((left, right, opp)):
            big_a1[k].append(same(f, mine, 4 + k, along(1, 0), h))
            big_a1[k].append(same(f, mine, 7 + k, along(3, 0), h))
            big_a2[k].append(same(f, eighth(a_prev, 0, 48), 10 + k, along(1, 0), h))
            big_a2[k].append(same(f, eighth(a_next, 48, 48), 13 + k, along(3, 0), h))
            big_twin[k].append(same(f, half, 16 + k, sib, h))

    def start(copies):
        for copy in copies:
            copy.start()
            drains.append(copy.wait_send)

    def arrived(copies):
        for copy in copies:
            copy.wait_recv()

    all_first = fk_recv.at[pl.ds(1, NS - 1)]
    drains = [lambda: rcopy(all_first, all_first, fk_ss, fk_rs.at[0], me, right).wait_send()]
    for copy in [out_local] + big_local:
        copy.start()
    start(big_x1)

    for r in range(KD // 128):
        kc = jnp.broadcast_to(kept8[r:r + 1], (128, 128)).T
        sender = kc & (ND - 1)
        s_seq, s_head = lax.shift_right_arithmetic(sender, 2), sender & (NH - 1)
        within = lax.shift_right_arithmetic(kc, 7) - lax.shift_right_arithmetic(first - sender + (ND - 1), 7)
        way = (lax.shift_right_arithmetic(s_seq, 3) - ypos) & 3
        way = way * 4 + ((lax.shift_right_arithmetic(s_seq, 1) - zpos) & 3)
        words = [sum(CHIPS.index(divmod(8 * half + k, 4)) << (4 * k) for k in range(7)) for half in (0, 1)]
        last = [CHIPS.index(divmod(8 * half + 7, 4)) for half in (0, 1)]
        place = lax.shift_right_arithmetic(jnp.where(way < 8, words[0], words[1]), (way & 7) * 4) & 15
        place = jnp.where((way & 7) == 7, jnp.where(way < 8, last[0], last[1]), place)
        rel = place * 2 + ((s_seq + core) & 1)
        slot[r * 128:(r + 1) * 128] = (
            lax.shift_right_arithmetic(rel, 2) * (PER * NH) + s_head * PER + (rel & (PER - 1))
        ) * WIN + within

    feat_load.wait()

    def send_windows(g):
        lo = 1 if g == 0 else 0
        firsts = fk_recv.at[pl.ds(g * PER + lo, PER - lo)]
        rcopy(firsts, firsts, fk_ss, fk_rs.at[g], me, right).wait_recv()
        start = lax.shift_right_arithmetic(fk_recv[g * PER:(g + 1) * PER] - source + (ND - 1), 7)
        start = jnp.concatenate([start, start], axis=1).reshape(GROWS, 128)
        want = start + iota((GROWS, 128), 0) % WIN - iota((GROWS, 128), 1)
        pick = jnp.concatenate(
            [(want == t * 128).astype(F32).astype(BF) for t in range(ROWS // 128)], axis=1
        )
        send[g * GROWS:(g + 1) * GROWS] = dot(pick, feat[...]).astype(BF)
        for i in range(lo, PER):
            rcopy(
                send.at[pl.ds(g * GROWS + i * WIN, WIN)], recv.at[g, h, pl.ds(i * WIN, WIN)],
                s1_ss, s1_rs.at[g], offset(g * PER + i, -1), h,
            ).start()
        if g == 0:
            recv[0, h, 0:WIN] = send[0:WIN]

    sent = send.at[pl.ds(WIN, (NS - 1) * WIN)]
    drains.append(lambda: rcopy(sent, sent, s1_ss, s1_rs.at[0], me, right).wait_send())

    def arrive(g):
        lo = WIN if g == 0 else 0
        part = recv.at[g, h, pl.ds(lo, GROWS - lo)]
        rcopy(part, part, s1_ss, s1_rs.at[g], me, right).wait_recv()

    rings = []
    for g in range(GROUPS):
        rings.append((
            rcopy(recv.at[g, h], recv.at[g, h], xs.at[g, 0], xr.at[g, 0], me, right),
            rcopy(recv.at[g, h], recv.at[g, h], xs.at[g, 1], xr.at[g, 1], me, left),
            rcopy(recv.at[g, left, pl.ds(0, GROWS // 2)], recv.at[g, left, pl.ds(0, GROWS // 2)], xs.at[g, 2], xr.at[g, 2], me, right),
            rcopy(recv.at[g, right, pl.ds(GROWS // 2, GROWS // 2)], recv.at[g, right, pl.ds(GROWS // 2, GROWS // 2)], xs.at[g, 3], xr.at[g, 3], me, left),
        ))

    def compact(g):
        for k in (2 * g, 2 * g + 1):
            rings[k][2].wait_recv()
            rings[k][3].wait_recv()

        def block(b, c):
            at = pl.ds(pl.multiple_of(b * 512, 512), 512)
            want = slot[at] - g * 512 - iota((512, 128), 1)
            pick = jnp.concatenate([(want == t * 128).astype(F32).astype(BF) for t in range(4)], axis=1)
            got = dot(pick, recv[2 * g:2 * g + 2].reshape(512, D))
            if g == 0:
                dense[at] = got
            else:
                dense[at] = dense[at] + got
            return c

        lax.fori_loop(0, KD // 512, block, 0)

    def ring_pass(g):
        rings[g][0].wait_recv()
        rings[g][2].start()
        rings[g][1].wait_recv()
        rings[g][3].start()

    drains += [copy.wait_send for ring in rings for copy in ring]
    def ring_start(g):
        arrive(g)
        rings[g][0].start()
        rings[g][1].start()

    send_windows(0)
    send_windows(1)
    ring_start(0)
    send_windows(2)
    ring_start(1)
    send_windows(3)
    send_windows(4)
    ring_pass(0)
    ring_start(2)
    send_windows(5)
    send_windows(6)
    ring_pass(1)
    ring_start(3)
    send_windows(7)
    ring_pass(2)
    ring_start(4)
    arrived(big_x1)
    start(big_a1[0] + big_a1[1])
    qkv_load.wait()
    for j in range(HPD):
        low, high = j * 128, j * 128 + 64
        rows = slice(j * 64, j * 64 + 64)
        at_q, at_0 = (high, low) if v_first(j) else (low, high)
        wqkv[at_0:at_0 + 64] = jnp.zeros((64, D), BF)
        wqkv[at_q:at_q + 64] = (wraw[0, rows].astype(F32) * 0.125).astype(BF)
        wqkv[384 + at_q:384 + at_q + 64] = wraw[1, rows]
        wqkv[384 + at_0:384 + at_0 + 64] = wraw[2, rows]

    def turn(parts):
        for k in parts:
            at = slice(k * 128, (k + 1) * 128)
            wturn[:, at] = wqkv[at].astype(F32).T.astype(BF)

    turn((0, 1, 2))
    ring_pass(3)
    ring_start(5)
    turn((3, 4, 5))
    ring_pass(4)
    ring_start(6)
    ring_pass(5)
    ring_start(7)
    compact(0)
    arrived(big_a1[0] + big_a1[1])
    start(big_a2[0] + big_a2[1])
    ring_pass(6)
    compact(1)
    ring_pass(7)
    start(big_x2)
    start(out_mine)
    arrived(big_a2[0] + big_a2[1])
    start(big_twin[0] + big_twin[1])
    compact(2)
    compact(3)

    def norm(blk, c):
        block = layer_norm(dense[pl.ds(pl.multiple_of(blk * 256, 256), 256)], again).astype(BF)
        normed[pl.ds(pl.multiple_of(blk * 256, 256), 256)] = block
        row = iota((48, 256), 0)
        which = jnp.where(row < 16, foff[0], jnp.where(row < 32, foff[1], foff[2]))
        sel = (iota((48, 256), 1) == (row & 15) * 16 + which).astype(F32).astype(BF)
        rows = dot(sel, block).astype(BF)
        for j in range(HPD):
            nfar[j, pl.ds(pl.multiple_of(blk * 16, 16), 16)] = rows[j * 16:(j + 1) * 16]
        return c

    lax.fori_loop(0, KD // 256, norm, 0)
    for j in range(HPD):
        cols = slice(j * 128, (j + 1) * 128)
        farkv[core, ypos, zpos, :, cols] = dot(nfar[j], wturn[:, 384 + j * 128:512 + j * 128]).astype(BF)

    def far_copy(at, k, seq):
        return rcopy(farkv.at[at], farkv.at[at], fs.at[k], fr.at[k], seq, h)

    spots = (zpos, z_prev, z_next, (zpos + 2) % 4)
    far_a1 = [far_copy((core, ypos, zpos), 0, across(0, 1)), far_copy((core, ypos, zpos), 1, across(0, 3))]
    far_a2 = [
        far_copy((core, ypos, z_prev, pl.ds(0, 32)), 2, across(0, 1)),
        far_copy((core, ypos, z_next, pl.ds(32, 32)), 3, across(0, 3)),
    ]
    far_b1 = [
        [far_copy((core, ypos, x), 4 + 2 * k, across(1, 0)), far_copy((core, ypos, x), 5 + 2 * k, across(3, 0))]
        for k, x in enumerate(spots)
    ]
    far_b2 = [
        [
            far_copy((core, y_prev, x, pl.ds(0, 32)), 12 + 2 * k, across(1, 0)),
            far_copy((core, y_next, x, pl.ds(32, 32)), 13 + 2 * k, across(3, 0)),
        ]
        for k, x in enumerate(spots)
    ]
    far_twin = [far_copy((core, at), 20 + k, sib) for k, at in enumerate((ypos, y_prev, y_next, (ypos + 2) % 4))]
    mid_z = rcopy(midkv.at[core, zbit], midkv.at[core, zbit], ms.at[0], mr.at[0], zpart, h)
    mid_s = rcopy(midkv.at[core], midkv.at[core], ms.at[1], mr.at[1], sib, h)
    start(far_a1 + far_b1[0])

    def project_kv(blk, c):
        at = pl.ds(pl.multiple_of(blk * 512, 512), 512)
        kvb = dot(normed[at], wturn[:, 384:]).astype(BF)
        kv[at] = kvb
        at_m = pl.ds(pl.multiple_of(blk * 128, 128), 128)
        for j in range(HPD):
            cols = slice(j * 128, (j + 1) * 128)
            sel = (iota((128, 512), 1) == iota((128, 512), 0) * 4 + moff[j]).astype(F32).astype(BF)
            midkv[core, zbit, at_m, cols] = dot(sel, kvb[:, cols]).astype(BF)
        return c

    lax.fori_loop(0, KD // 512, project_kv, 0)
    start([mid_z])
    arrived(far_a1)
    start(far_a2 + far_b1[1] + far_b1[2])

    def project_q(blk, c):
        at = pl.ds(pl.multiple_of(blk * 512, 512), 512)
        qb = dot(normed[at], wturn[:, :384]).astype(BF)
        q[at] = qb
        at_m = pl.ds(pl.multiple_of(blk * 128, 128), 128)
        for j in range(HPD):
            cols = slice(j * 128, (j + 1) * 128)
            sel = (iota((128, 512), 1) == iota((128, 512), 0) * 4 + moff[j]).astype(F32).astype(BF)
            qmid[at_m, cols] = dot(sel, qb[:, cols]).astype(BF)
        return c

    lax.fori_loop(0, KD // 512, project_q, 0)
    for j in range(HPD):
        cols = slice(j * 128, (j + 1) * 128)
        qfar[:, cols] = dot(nfar[j], wturn[:, j * 128:(j + 1) * 128]).astype(BF)
    arrived(far_a2 + far_b1[0])
    start(far_b1[3] + far_b2[0] + far_twin[:1])

    def attend(qb, keys, j):
        scores = dot_nt(qb, keys)
        top = jnp.max(scores, axis=-1, keepdims=True)
        p = jnp.exp(scores - top)
        total = jnp.sum(p, axis=-1, keepdims=True)
        out = dot(p.astype(BF), keys)
        lane = iota(out.shape, 1)
        base = 64 if v_first(j) else 0
        out = jnp.where((lane >= base) & (lane < base + 32), top, out)
        return jnp.where((lane >= base + 32) & (lane < base + 64), total, out)

    def short(j, first_block):
        cols = slice(j * 128, (j + 1) * 128)

        at = slice(first_block * 256, first_block * 256 + 512)
        acc[j, at] = attend(q[at, cols], kv[:, cols], j)

    arrived(out_mine)
    start(out_ahead + out_twin[:2])
    short(0, 0)
    short(0, 2)
    arrived(far_b1[1] + far_b1[2])
    start(far_b2[1] + far_b2[2])
    short(1, 0)
    arrived(far_b1[3])
    start(far_b2[3] + far_twin[1:3])
    short(1, 2)
    arrived([mid_z])
    start([mid_s])
    arrived(out_ahead)
    start(out_twin[2:])
    short(2, 0)
    for k in range(4):
        arrived(far_b2[k])
    start(far_twin[3:])
    arrived(big_x2)
    start(big_a1[2])
    short(2, 2)
    arrived([mid_s])
    for j in range(HPD):
        cols = slice(j * 128, (j + 1) * 128)
        accm[j] = attend(qmid[:, cols], midkv[:, :, :, cols].reshape(KD, 128), j)
    arrived(far_twin)
    for j in range(HPD):
        cols = slice(j * 128, (j + 1) * 128)
        accf[j] = attend(qfar[:, cols], farkv[:, :, :, :, cols].reshape(2048, 128), j)

    def spread(one_hot, x):
        one = x.astype(BF)
        rest = x - one.astype(F32)
        two = rest.astype(BF)
        three = (rest - two.astype(F32)).astype(BF)
        return dot(one_hot, one) + dot(one_hot, two) + dot(one_hot, three)

    def merge(g):
        heads = []
        at = pl.ds(pl.multiple_of(g * 256, 256), 256)
        at_m = pl.ds(pl.multiple_of(g * 64, 64), 64)
        at_f = pl.ds(pl.multiple_of(g * 16, 16), 16)
        for j in range(HPD):
            base = 64 if v_first(j) else 0
            near = acc[j, at]
            hot_m = (iota((256, 64), 0) == iota((256, 64), 1) * 4 + moff[j]).astype(F32).astype(BF)
            hot_f = (iota((256, 16), 0) == iota((256, 16), 1) * 16 + foff[j]).astype(F32).astype(BF)
            middle = spread(hot_m, accm[j, at_m])
            far = spread(hot_f, accf[j, at_f])
            pos = iota((256, 1), 0)
            in_m = pos % 4 == moff[j]
            in_f = pos % 16 == foff[j]
            top_n = near[:, base:base + 1]
            top_m = jnp.where(in_m, middle[:, base:base + 1], NEG)
            top_f = jnp.where(in_f, far[:, base:base + 1], NEG)
            top = jnp.maximum(jnp.maximum(top_n, top_m), top_f)
            c_n = jnp.exp(top_n - top)
            c_m = jnp.exp(top_m - top)
            c_f = jnp.exp(top_f - top)
            under = (
                c_n * near[:, base + 32:base + 33]
                + c_m * middle[:, base + 32:base + 33]
                + c_f * far[:, base + 32:base + 33]
            )
            heads.append((c_n * near + c_m * middle + c_f * far) / under)
        lane = iota((256, 128), 1)
        lower = jnp.where(lane < 64, heads[0], heads[1])
        third = heads[2]
        upper = jnp.where(lane[:128] < 64, third[:128], pltpu.roll(third[128:], 64, 1))
        return lower.astype(BF), upper.astype(BF)

    swaps = []
    for r, g in enumerate((opp, right, left)):
        ho_send[r, :256], ho_send[r, 256:] = merge(g)
        swap = rcopy(ho_send.at[r], ho_recv.at[h], hs.at[r], hr.at[r], me, g)
        start([swap])
        swaps.append(swap)
        if r == 1:
            arrived(big_a1[2])
            start(big_a2[2])
    ho_recv[h, :256], ho_recv[h, 256:] = merge(h)
    out_local.wait()
    arrived(out_twin)
    attended = jnp.zeros((SHARE, D), F32)
    lane = iota((128, 128), 1)
    for g, swap in ((h, []), (left, swaps[1:2]), (right, swaps[2:]), (opp, swaps[:1])):
        arrived(swap)
        third = ho_recv[g, 256:]
        zero = jnp.zeros_like(third)
        third = jnp.concatenate([jnp.where(lane < 64, third, zero), jnp.where(lane < 64, zero, third)], axis=0)
        tail = outf[g, 128:]
        product = dot(ho_recv[g, :256], outf[g, :128]) + dot(third, jnp.concatenate([tail, tail], axis=0))
        attended = attended + product.astype(BF).astype(F32)
        if not swap:
            arrived(big_a2[2])
            start(big_twin[2])
    residual = dense[pl.ds(pl.multiple_of(h * SHARE, SHARE), SHARE)] + attended
    normed_two = layer_norm(residual, mgain).astype(BF)
    for copy in big_local:
        copy.wait()

    total = residual
    for g, twin in ((h, []), (left, big_twin[0]), (right, big_twin[1]), (opp, big_twin[2])):
        arrived(twin)
        hidden = dot(normed_two, upf[g])
        hidden = (0.5 * hidden * (1.0 + lax.erf(hidden * 0.7071067811865476))).astype(BF)
        total = total + dot(hidden, downf[g]).astype(BF).astype(F32)
    o_ref[...] = total.astype(BF)

    for drain in drains:
        drain()


def local(tile_features, kept_tiles, attn_gain, qkv_weight, out_weight, middle_head_offset,
          far_head_offset, mlp_gain, up_weight, down_weight):
    vmem = pl.BlockSpec(memory_space=pltpu.VMEM)
    smem = pl.BlockSpec(memory_space=pltpu.SMEM)
    hbm = pl.BlockSpec(memory_space=pl.ANY)
    dma = pltpu.SemaphoreType.DMA
    return pl.pallas_call(
        kernel,
        out_shape=jax.ShapeDtypeStruct((SHARE, D), BF),
        in_specs=[smem, smem, vmem, vmem, vmem, hbm, hbm, hbm, hbm, hbm],
        out_specs=vmem,
        scratch_shapes=[
            pltpu.VMEM((ROWS, D), BF),
            pltpu.VMEM((3, 192, D), BF),
            pltpu.VMEM((D, D), BF),
            pltpu.VMEM((D, D), BF),
            pltpu.VMEM((NS * WIN, D), BF),
            pltpu.VMEM((GROUPS, NH, GROWS, D), BF),
            pltpu.VMEM((KD, 128), jnp.int32),
            pltpu.VMEM((KD, D), F32),
            pltpu.VMEM((KD, 384), BF),
            pltpu.VMEM((KD, 384), BF),
            pltpu.VMEM((256, 384), BF),
            pltpu.VMEM((64, 384), BF),
            pltpu.VMEM((KD, D), BF),
            pltpu.VMEM((HPD, 64, D), BF),
            pltpu.VMEM((2, 2, 256, 384), BF),
            pltpu.VMEM((2, 4, 4, 64, 384), BF),
            pltpu.VMEM((HPD, KD, 128), F32),
            pltpu.VMEM((HPD, 256, 128), F32),
            pltpu.VMEM((HPD, 64, 128), F32),
            pltpu.VMEM((3, 384, 128), BF),
            pltpu.VMEM((NH, 384, 128), BF),
            pltpu.VMEM((8, 128), jnp.int32),
            pltpu.VMEM((NS, 8, 128), jnp.int32),
            pltpu.VMEM((NH, D, D), BF),
            pltpu.VMEM((NH, D, D), BF),
            pltpu.VMEM((NH, 192, D), BF),
            dma, dma((GROUPS,)), dma, dma((GROUPS,)), dma((GROUPS, 4)), dma((GROUPS, 4)), dma((7,)), dma((7,)), dma((2, 19)), dma((2, 19)),
            dma((3,)), dma((2,)), dma((2,)), dma((2,)), dma((24,)), dma((24,)), dma((3,)), dma((3,)),
        ],
        compiler_params=pltpu.CompilerParams(
            collective_id=0, has_side_effects=True, vmem_limit_bytes=56 * 1024 * 1024
        ),
        cost_estimate=pl.CostEstimate(flops=12_000_000_000, bytes_accessed=20_000_000, transcendentals=5_000_000),
    )(
        middle_head_offset, far_head_offset, kept_tiles.reshape(8, 128), attn_gain.reshape(6, 128),
        mlp_gain.reshape(6, 128), tile_features, qkv_weight.transpose(1, 2, 0), up_weight, down_weight, out_weight,
    )


def solution(mesh):
    in_specs = (
        P(("seq", "head"), None),
        P("seq"),
        P(),
        P(None, None, "head"),
        P("head", None),
        P("head"),
        P("head"),
        P(),
        P(None, "head"),
        P("head", None),
    )
    out_specs = P(("seq", "head"), None)
    return jax.shard_map(local, mesh=mesh, in_specs=in_specs, out_specs=out_specs, check_vma=False)
```
